32 devices in a mesh: dp: 4 (over z), ctx: 4 (over y, x), chan: 2 (over core).
Axes of the slice: x: 2, y: 2, z: 4, core: 2. Of those that a mesh axis runs over, the one named last changes fastest.
Arguments:
- layer_input: bfloat16 [4096, 4096], P(('dp', 'chan'), 'ctx'), may hold values from -6 to 6
- grad_output: bfloat16 [4096, 4096], P(('dp', 'chan'), 'ctx'), may hold values from -6 to 6
- filter_taps: float32 [8, 512, 4096], P(('dp', 'chan'), 'ctx'), may hold values from -2 to 2
Outputs:
- grad_input: bfloat16 [4096, 4096], P(('dp', 'chan'), 'ctx')
- grad_filter: float32 [8, 512, 4096], P(('dp', 'chan'), 'ctx')
The draws below stay inside these ranges and needn't reach their ends.
All inputs are finite; a program needn't handle non-finite values.
Results may differ from the reference program's by a relative error of at most 0.001.
Values may be sent and summed in bfloat16 or wider, within the bound.
No kernel may reach another device: no remote copies, remote signals or barrier semaphores. Data moves between devices by JAX's collectives and lax.ppermute only.
A program may use at most 128 MiB of HBM per device.

```python
import math
import jax
import jax.numpy as jnp
from jax import lax

CHANNELS = 4096
LENGTH = 4096
CHAN_DEV = 512


def draw_filter_taps(key, part):
    key_rate, key_pick, key_noise, key_lag = jax.random.split(key, 4)
    group_count = CHANNELS // CHAN_DEV
    kernel_coefficient_dims = (group_count, CHAN_DEV, LENGTH)
    slow_low = math.log(0.25 / LENGTH)
    slow_high = math.log(2.0 / LENGTH)
    fast_high = math.log(1.0 / 20.0)
    pick = jax.random.uniform(key_pick, (group_count, CHAN_DEV, 1), jnp.float32)
    unit = jax.random.uniform(key_rate, (group_count, CHAN_DEV, 1), jnp.float32)
    slow_rate = jnp.exp(slow_low + unit * (slow_high - slow_low))
    fast_rate = jnp.exp(slow_high + unit * (fast_high - slow_high))
    slow_share = 0.5
    gaussian_perturbation = jnp.clip(jax.random.normal(key_noise, kernel_coefficient_dims, jnp.float32), -4.0, 4.0)
    fading_speed = jnp.where(pick < slow_share, slow_rate, fast_rate)
    lag_position = lax.broadcasted_iota(jnp.int32, kernel_coefficient_dims, 2)
    lag_shifts = jax.random.randint(key_lag, (3, group_count, CHAN_DEV, 1), 1, LENGTH)
    spike_height = jnp.ones(kernel_coefficient_dims, jnp.float32)
    for batch_members in range(3):
        spike_height = spike_height * jnp.where(lag_position >= lag_shifts[batch_members], 0.6, 1.0)
    fading_multiplier = jnp.exp(-fading_speed * lag_position.astype(jnp.float32))
    kernel_coefficients = jnp.sqrt(2.0 * fading_speed) * fading_multiplier * gaussian_perturbation * spike_height
    return kernel_coefficients.astype(jnp.float32)


def block_levels(own_key, shape, shards, least, top_value):
    factor_of = 1.0
    for axis_at, parts in shards:
        draws = jax.random.uniform(jax.random.fold_in(jax.random.fold_in(own_key, 6), axis_at), (parts,), jnp.float32, least / len(shards), top_value / len(shards))
        factor_of = factor_of * jnp.repeat(jnp.exp(draws), shape[axis_at] // parts).reshape((-1,) + (1,) * (len(shape) - 1 - axis_at))
    return factor_of


def noise(stream_key, dims, deviation, reach, cuts=(), kind=jnp.bfloat16):
    entries = deviation * jax.random.normal(stream_key, dims, jnp.float32)
    if cuts:
        entries = entries * block_levels(stream_key, dims, cuts, -0.22, 0.18)
    return jnp.clip(entries, -reach, reach).astype(kind)


def setup_inputs(seed: int = 0) -> dict:
    streams_of = jax.random.split(jax.random.key(seed), 4)
    layer_input = noise(streams_of[0], (CHANNELS, LENGTH), 1.0, 6.0, ((0, 8), (1, 4)))
    grad_output = noise(streams_of[1], (CHANNELS, LENGTH), 1.0, 6.0, ((0, 8), (1, 4)))
    filter_taps = draw_filter_taps(jax.random.fold_in(streams_of[3], 71), 0)
    return dict(layer_input=layer_input, grad_output=grad_output, filter_taps=filter_taps)


def reference(layer_input, grad_output, filter_taps):
    size_fft = 2 * LENGTH
    block = min(256, CHANNELS)
    block_count = CHANNELS // block
    taps = filter_taps.reshape(block_count, block, LENGTH)
    inputs = layer_input.reshape(block_count, block, LENGTH)
    grads = grad_output.reshape(block_count, block, LENGTH)

    def one_block(pieces):
        input_rows, grad_rows, filter_rows = pieces
        input_spec = jnp.fft.rfft(input_rows.astype(jnp.float32), n=size_fft, axis=1)
        grad_spec = jnp.fft.rfft(grad_rows.astype(jnp.float32), n=size_fft, axis=1)
        filter_spec = jnp.fft.rfft(filter_rows, n=size_fft, axis=1)
        back = jnp.fft.irfft(jnp.conj(filter_spec) * grad_spec, n=size_fft, axis=1)[:, :LENGTH]
        corr = jnp.fft.irfft(grad_spec * jnp.conj(input_spec), n=size_fft, axis=1)[:, :LENGTH]
        return (back.astype(jnp.bfloat16), (corr / math.sqrt(LENGTH)).astype(jnp.float32))
    grad_input, grad_filter = lax.map(one_block, (inputs, grads, taps))
    grad_input = grad_input.reshape(CHANNELS, LENGTH)
    grad_filter = grad_filter.reshape(filter_taps.shape)
    return (grad_input, grad_filter)
```

```python
import functools
import math

import jax
import jax.numpy as jnp
import ml_dtypes
import numpy as np
from jax import lax
from jax.experimental import pallas as pl
from jax.experimental.pallas import tpu as pltpu
from jax.sharding import PartitionSpec as P

LANES = 128
TILE = 16
HALF_TILE = 8


def split_table(table):
    high = table.astype(ml_dtypes.bfloat16)
    low = (table - high.astype(np.float64)).astype(ml_dtypes.bfloat16)
    return high, low


def dft_tables(length):
    index = np.arange(LANES)
    angle = 2.0 * np.pi * (np.outer(index, index) % LANES) / LANES
    cos, sin = np.cos(angle), np.sin(angle)
    ahead = np.block([[cos, -sin], [sin, cos]])
    back = np.block([[cos, sin], [-sin, cos]]) / length
    outer = length // LANES
    order = np.concatenate([np.arange(0, outer, 2), np.arange(1, outer, 2)])
    turn = 2.0 * np.pi * np.outer(order + 0.25, index) / length
    twiddle = np.stack([np.cos(turn), np.sin(turn)], axis=1).astype(np.float32)
    return split_table(ahead), split_table(back), split_table(back / math.sqrt(length)), twiddle


def add(a, b):
    return (a[0] + b[0], a[1] + b[1])


def sub(a, b):
    return (a[0] - b[0], a[1] - b[1])


def turn_quarter(a, sign):
    return (-a[1], a[0]) if sign > 0 else (a[1], -a[0])


def turn_by(a, numerator, denominator, sign):
    numerator = numerator % denominator
    if numerator == 0:
        return a
    if 4 * numerator == denominator:
        return turn_quarter(a, sign)
    if 2 * numerator == denominator:
        return (-a[0], -a[1])
    if 4 * numerator == 3 * denominator:
        return turn_quarter(a, -sign)
    angle = sign * 2.0 * math.pi * numerator / denominator
    cos, sin = math.cos(angle), math.sin(angle)
    if 8 * numerator % denominator == 0:
        root = math.sqrt(0.5)
        re, im = a
        if cos * sin > 0:
            re, im = re - im, re + im
        else:
            re, im = re + im, im - re
        return (re * (root if cos > 0 else -root), im * (root if cos > 0 else -root))
    return (a[0] * cos - a[1] * sin, a[0] * sin + a[1] * cos)


def fft(points, sign):
    count = len(points)
    if count == 1:
        return points
    if count == 2:
        return [add(points[0], points[1]), sub(points[0], points[1])]
    if count % 4:
        evens, odds = fft(points[0::2], sign), fft(points[1::2], sign)
        turned = [turn_by(odds[k], k, count, sign) for k in range(count // 2)]
        return [add(a, b) for a, b in zip(evens, turned)] + [sub(a, b) for a, b in zip(evens, turned)]
    quarter = count // 4
    parts = [fft(points[r::4], sign) for r in range(4)]
    out = [None] * count
    for k in range(quarter):
        p0, p1, p2, p3 = (turn_by(parts[r][k], r * k, count, sign) for r in range(4))
        s02, d02, s13, d13 = add(p0, p2), sub(p0, p2), add(p1, p3), sub(p1, p3)
        out[k] = add(s02, s13)
        out[k + 2 * quarter] = sub(s02, s13)
        if sign > 0:
            out[k + quarter] = (d02[0] - d13[1], d02[1] + d13[0])
            out[k + 3 * quarter] = (d02[0] + d13[1], d02[1] - d13[0])
        else:
            out[k + quarter] = (d02[0] + d13[1], d02[1] - d13[0])
            out[k + 3 * quarter] = (d02[0] - d13[1], d02[1] + d13[0])
    return out


def outer_forward(load, store, twiddle_ref, outer, half):
    count = outer // 2
    for row in range(0, TILE, HALF_TILE):
        points = []
        for n in range(count):
            near = -2.0 * math.pi * n * (half + 0.25) / outer
            far = -2.0 * math.pi * (n + count) * (half + 0.25) / outer
            a, b = load(n, row), load(n + count, row)
            if n == 0:
                points.append((a + b * math.cos(far), b * math.sin(far)))
            else:
                points.append((a * math.cos(near) + b * math.cos(far), a * math.sin(near) + b * math.sin(far)))
        for k, (re, im) in enumerate(fft(points, -1)):
            at = half * count + k
            cos, sin = twiddle_ref[at, 0:1, :], twiddle_ref[at, 1:2, :]
            store(at, row, re * cos + im * sin, im * cos - re * sin)


def outer_inverse(spec_ref, twiddle_ref, out_ref, outer, half):
    count = outer // 2
    for row in range(0, TILE, HALF_TILE):
        points = []
        for k in range(count):
            at = half * count + k
            rows = pl.ds(at * TILE + row, HALF_TILE)
            re, im = spec_ref[rows, 0:LANES], spec_ref[rows, LANES : 2 * LANES]
            cos, sin = twiddle_ref[at, 0:1, :], twiddle_ref[at, 1:2, :]
            points.append((re * cos - im * sin, re * sin + im * cos))
        for n, (re, im) in enumerate(fft(points, 1)):
            for place in (n, n + count):
                angle = 2.0 * math.pi * place * (half + 0.25) / outer
                value = re if place == 0 else re * math.cos(angle) - im * math.sin(angle)
                if half == 0:
                    out_ref[place, row : row + HALF_TILE, :] = value
                else:
                    out_ref[place, row : row + HALF_TILE, :] += value


def matmul(values, high_ref, low_ref):
    high = values.astype(jnp.bfloat16)
    low = (values - high.astype(jnp.float32)).astype(jnp.bfloat16)
    dot = functools.partial(jnp.dot, preferred_element_type=jnp.float32)
    return dot(high, high_ref[...]) + dot(low, high_ref[...]) + dot(high, low_ref[...])


def spectrum_kernel(taps_ref, ahead_high, ahead_low, twiddle_ref, spec_ref, work_ref, *, outer):
    count = outer // 2

    def load(n, row):
        return taps_ref[row : row + HALF_TILE, n * LANES : (n + 1) * LANES]

    def store(at, row, re, im):
        rows = pl.ds(at * TILE + row, HALF_TILE)
        work_ref[rows, 0:LANES] = re
        work_ref[rows, LANES : 2 * LANES] = im

    for half in range(2):
        outer_forward(load, store, twiddle_ref, outer, half)
    for half in range(2):
        rows = pl.ds(half * count * TILE, count * TILE)
        spec_ref[0, rows, :] = matmul(work_ref[rows, :], ahead_high, ahead_low)


def correlate(piece_refs, me, mate_ref, keep_ref, signal_is_grad, tables, fill_ref, work_ref, out_ref, outer):
    ahead_high, ahead_low, back_high, back_low, twiddle_ref = tables
    count = outer // 2
    per_piece = outer // len(piece_refs)
    for k, ref in enumerate(piece_refs):
        first = (me ^ k) * per_piece
        for i in range(per_piece):
            fill_ref[first + i] = ref[:, i * LANES : (i + 1) * LANES].astype(jnp.float32)

    def load(n, row):
        return fill_ref[n, row : row + HALF_TILE, :]

    def store(at, row, re, im):
        rows = pl.ds(at * TILE + row, HALF_TILE)
        work_ref[rows, 0:LANES] = re
        work_ref[rows, LANES : 2 * LANES] = im

    for half in range(2):
        outer_forward(load, store, twiddle_ref, outer, half)
    for half in range(2):
        rows = pl.ds(half * count * TILE, count * TILE)
        own = matmul(work_ref[rows, :], ahead_high, ahead_low)
        if keep_ref is not None:
            keep_ref[0, rows, :] = own
        mate = mate_ref[0, rows, :]
        grad, other = (own, mate) if signal_is_grad else (mate, own)
        grad_re, grad_im = grad[:, :LANES], grad[:, LANES:]
        other_re, other_im = other[:, :LANES], other[:, LANES:]
        both = jnp.concatenate(
            [other_re * grad_re + other_im * grad_im, other_re * grad_im - other_im * grad_re], axis=1
        )
        work_ref[rows, :] = matmul(both, back_high, back_low)
    for half in range(2):
        outer_inverse(work_ref, twiddle_ref, out_ref, outer, half)


def input_kernel(me_ref, *refs, outer, parts):
    pieces, (mate_ref, *tables) = refs[:parts], refs[parts : parts + 6]
    keep_ref, *sends = refs[parts + 6 : 2 * parts + 7]
    fill_ref, work_ref, out_ref = refs[2 * parts + 7 :]
    me = me_ref[0]
    correlate(pieces, me, mate_ref, keep_ref, True, tables, fill_ref, work_ref, out_ref, outer)
    per_piece = outer // parts
    for k, ref in enumerate(sends):
        first = (me ^ k) * per_piece
        for i in range(per_piece):
            ref[:, i * LANES : (i + 1) * LANES] = out_ref[first + i].astype(jnp.bfloat16)


def filter_kernel(me_ref, *refs, outer, parts):
    pieces, (mate_ref, *tables) = refs[:parts], refs[parts : parts + 6]
    result_ref, fill_ref, work_ref, out_ref = refs[parts + 6 :]
    correlate(pieces, me_ref[0], mate_ref, None, False, tables, fill_ref, work_ref, out_ref, outer)
    for n in range(outer):
        result_ref[:, n * LANES : (n + 1) * LANES] = out_ref[n]


def gather_kernel(me_ref, *refs, pencil):
    *pieces, out_ref, sems = refs
    copies = []
    for k, ref in enumerate(pieces):
        rows = pl.ds((me_ref[0] ^ k) * pencil, pencil)
        copies.append(pltpu.make_async_copy(ref, out_ref.at[rows, :], sems.at[k]))
    for copy in copies:
        copy.start()
    for copy in copies:
        copy.wait()


def shards(layer_input, grad_output, filter_taps):
    parts = lax.axis_size("ctx")
    me = lax.axis_index("ctx")
    pencil, piece = layer_input.shape[0] // parts, layer_input.shape[1]
    length = piece * parts
    outer = length // LANES
    aligned = pencil % TILE == 0
    rows = -(-pencil // TILE) * TILE
    steps = rows // TILE
    ahead, back, back_scaled, twiddle = dft_tables(length)
    me_array = me.astype(jnp.int32).reshape(1)

    def swap(block, k):
        return lax.ppermute(block, "ctx", [(i, i ^ k) for i in range(parts)])

    def pick(array, k):
        blocks = array.reshape(parts, pencil, piece)
        return lax.dynamic_index_in_dim(blocks, me ^ k, 0, keepdims=False)

    def pad(block):
        return block if aligned else jnp.pad(block, ((0, rows - pencil), (0, 0)))

    whole = lambda array: pl.BlockSpec(array.shape, lambda s, *_: (0,) * array.ndim)
    piece_spec = pl.BlockSpec((TILE, piece), lambda s, *_: (s, 0))
    own_spec = pl.BlockSpec((TILE, piece), lambda s, at: (at[0] * steps + s, 0)) if aligned else piece_spec
    full_spec = pl.BlockSpec((TILE, length), lambda s, *_: (s, 0))
    spec_spec = pl.BlockSpec((1, outer * TILE, 2 * LANES), lambda s, *_: (s, 0, 0))
    spec_shape = jax.ShapeDtypeStruct((steps, outer * TILE, 2 * LANES), jnp.float32)
    work = pltpu.VMEM((outer * TILE, 2 * LANES), jnp.float32)
    lane_tiles = pltpu.VMEM((outer, TILE, LANES), jnp.float32)
    params = pltpu.CompilerParams(vmem_limit_bytes=32 * 1024 * 1024)
    stage_flops = 2 * 3 * rows * outer * (2 * LANES) ** 2
    spec_bytes = 4 * rows * length * 2

    def cost(stages, moved):
        return pl.CostEstimate(flops=stages * stage_flops, bytes_accessed=moved, transcendentals=0)

    def own_of(array):
        return array if aligned else pad(pick(array, 0))

    grad_pieces = [swap(pick(grad_output, k), k) for k in range(1, parts)]
    input_pieces = [swap(pick(layer_input, k), k) for k in range(1, parts)]

    taps = pad(filter_taps.reshape(pencil, length))
    taps_spectrum = pl.pallas_call(
        functools.partial(spectrum_kernel, outer=outer),
        grid=(steps,),
        in_specs=[full_spec, whole(ahead[0]), whole(ahead[1]), whole(twiddle)],
        out_specs=spec_spec,
        out_shape=spec_shape,
        scratch_shapes=[work],
        compiler_params=params,
        cost_estimate=cost(1, 2 * spec_bytes),
        name="taps_spectrum",
    )(taps, *ahead, twiddle)

    tables = [*ahead, *back, twiddle]
    grad_spectrum, *outgoing = pl.pallas_call(
        functools.partial(input_kernel, outer=outer, parts=parts),
        grid_spec=pltpu.PrefetchScalarGridSpec(
            num_scalar_prefetch=1,
            grid=(steps,),
            in_specs=[own_spec, *[piece_spec] * (parts - 1), spec_spec, *map(whole, tables)],
            out_specs=[spec_spec, *[piece_spec] * parts],
            scratch_shapes=[lane_tiles, work, lane_tiles],
        ),
        out_shape=[spec_shape, *[jax.ShapeDtypeStruct((rows, piece), jnp.bfloat16)] * parts],
        compiler_params=params,
        cost_estimate=cost(2, 2 * spec_bytes),
        name="grad_input",
    )(me_array, own_of(grad_output), *map(pad, grad_pieces), taps_spectrum, *tables)

    incoming = [outgoing[0][:pencil]] + [swap(outgoing[k][:pencil], k) for k in range(1, parts)]

    tables = [*ahead, *back_scaled, twiddle]
    grad_filter = pl.pallas_call(
        functools.partial(filter_kernel, outer=outer, parts=parts),
        grid_spec=pltpu.PrefetchScalarGridSpec(
            num_scalar_prefetch=1,
            grid=(steps,),
            in_specs=[own_spec, *[piece_spec] * (parts - 1), spec_spec, *map(whole, tables)],
            out_specs=full_spec,
            scratch_shapes=[lane_tiles, work, lane_tiles],
        ),
        out_shape=jax.ShapeDtypeStruct((rows, length), jnp.float32),
        compiler_params=params,
        cost_estimate=cost(2, 2 * spec_bytes),
        name="grad_filter",
    )(me_array, own_of(layer_input), *map(pad, input_pieces), grad_spectrum, *tables)

    if aligned:
        grad_input = pl.pallas_call(
            functools.partial(gather_kernel, pencil=pencil),
            in_specs=[pl.BlockSpec(memory_space=pltpu.SMEM), *[pl.BlockSpec(memory_space=pl.ANY)] * parts],
            out_specs=pl.BlockSpec(memory_space=pl.ANY),
            out_shape=jax.ShapeDtypeStruct((parts * pencil, piece), jnp.bfloat16),
            scratch_shapes=[pltpu.SemaphoreType.DMA((parts,))],
            name="gather_pieces",
        )(me_array, *incoming)
    else:
        slots = jnp.zeros((parts, pencil, piece), jnp.bfloat16)
        for k, block in enumerate(incoming):
            slots = lax.dynamic_update_index_in_dim(slots, block, me ^ k, 0)
        grad_input = slots.reshape(parts * pencil, piece)
    return (grad_input, grad_filter[:pencil].reshape(1, pencil, length))


def solution(mesh):
    in_specs = (P(("dp", "chan"), "ctx"), P(("dp", "chan"), "ctx"), P(("dp", "chan"), "ctx", None))
    out_specs = (P(("dp", "chan"), "ctx"), P(("dp", "chan"), "ctx", None))
    return jax.shard_map(shards, mesh=mesh, in_specs=in_specs, out_specs=out_specs, check_vma=False)
```

```python
import functools
import math

import jax
import jax.numpy as jnp
import ml_dtypes
import numpy as np
from jax import lax
from jax.experimental import pallas as pl
from jax.experimental.pallas import tpu as pltpu
from jax.sharding import PartitionSpec as P

LANES = 128
TILE = 16
HALF_TILE = 8


def split_table(table):
    high = table.astype(ml_dtypes.bfloat16)
    low = (table - high.astype(np.float64)).astype(ml_dtypes.bfloat16)
    return high, low


def dft_tables(length):
    index = np.arange(LANES)
    angle = 2.0 * np.pi * (np.outer(index, index) % LANES) / LANES
    cos, sin = np.cos(angle), np.sin(angle)
    ahead = np.block([[cos, -sin], [sin, cos]])
    back = np.block([[cos, sin], [-sin, cos]]) / length
    outer = length // LANES
    order = np.concatenate([np.arange(0, outer, 2), np.arange(1, outer, 2)])
    turn = 2.0 * np.pi * np.outer(order + 0.25, index) / length
    twiddle = np.stack([np.cos(turn), np.sin(turn)], axis=1).astype(np.float32)
    return split_table(ahead), split_table(back), split_table(back / math.sqrt(length)), twiddle


def add(a, b):
    return (a[0] + b[0], a[1] + b[1])


def sub(a, b):
    return (a[0] - b[0], a[1] - b[1])


def turn_quarter(a, sign):
    return (-a[1], a[0]) if sign > 0 else (a[1], -a[0])


def turn_by(a, numerator, denominator, sign):
    numerator = numerator % denominator
    if numerator == 0:
        return a
    if 4 * numerator == denominator:
        return turn_quarter(a, sign)
    if 2 * numerator == denominator:
        return (-a[0], -a[1])
    if 4 * numerator == 3 * denominator:
        return turn_quarter(a, -sign)
    angle = sign * 2.0 * math.pi * numerator / denominator
    cos, sin = math.cos(angle), math.sin(angle)
    if 8 * numerator % denominator == 0:
        root = math.sqrt(0.5)
        re, im = a
        if cos * sin > 0:
            re, im = re - im, re + im
        else:
            re, im = re + im, im - re
        return (re * (root if cos > 0 else -root), im * (root if cos > 0 else -root))
    return (a[0] * cos - a[1] * sin, a[0] * sin + a[1] * cos)


def fft(points, sign):
    count = len(points)
    if count == 1:
        return points
    if count == 2:
        return [add(points[0], points[1]), sub(points[0], points[1])]
    if count % 4:
        evens, odds = fft(points[0::2], sign), fft(points[1::2], sign)
        turned = [turn_by(odds[k], k, count, sign) for k in range(count // 2)]
        return [add(a, b) for a, b in zip(evens, turned)] + [sub(a, b) for a, b in zip(evens, turned)]
    quarter = count // 4
    parts = [fft(points[r::4], sign) for r in range(4)]
    out = [None] * count
    for k in range(quarter):
        p0, p1, p2, p3 = (turn_by(parts[r][k], r * k, count, sign) for r in range(4))
        s02, d02, s13, d13 = add(p0, p2), sub(p0, p2), add(p1, p3), sub(p1, p3)
        out[k] = add(s02, s13)
        out[k + 2 * quarter] = sub(s02, s13)
        if sign > 0:
            out[k + quarter] = (d02[0] - d13[1], d02[1] + d13[0])
            out[k + 3 * quarter] = (d02[0] + d13[1], d02[1] - d13[0])
        else:
            out[k + quarter] = (d02[0] + d13[1], d02[1] - d13[0])
            out[k + 3 * quarter] = (d02[0] - d13[1], d02[1] + d13[0])
    return out


def outer_forward(load, store, twiddle_ref, outer, half):
    count = outer // 2
    for row in range(0, TILE, HALF_TILE):
        points = []
        for n in range(count):
            near = -2.0 * math.pi * n * (half + 0.25) / outer
            far = -2.0 * math.pi * (n + count) * (half + 0.25) / outer
            a, b = load(n, row), load(n + count, row)
            if n == 0:
                points.append((a + b * math.cos(far), b * math.sin(far)))
            else:
                points.append((a * math.cos(near) + b * math.cos(far), a * math.sin(near) + b * math.sin(far)))
        for k, (re, im) in enumerate(fft(points, -1)):
            at = half * count + k
            cos, sin = twiddle_ref[at, 0:1, :], twiddle_ref[at, 1:2, :]
            store(at, row, re * cos + im * sin, im * cos - re * sin)


def outer_inverse(spec_ref, twiddle_ref, out_ref, outer, half):
    count = outer // 2
    for row in range(0, TILE, HALF_TILE):
        points = []
        for k in range(count):
            at = half * count + k
            rows = pl.ds(at * TILE + row, HALF_TILE)
            re, im = spec_ref[rows, 0:LANES], spec_ref[rows, LANES : 2 * LANES]
            cos, sin = twiddle_ref[at, 0:1, :], twiddle_ref[at, 1:2, :]
            points.append((re * cos - im * sin, re * sin + im * cos))
        for n, (re, im) in enumerate(fft(points, 1)):
            for place in (n, n + count):
                angle = 2.0 * math.pi * place * (half + 0.25) / outer
                value = re if place == 0 else re * math.cos(angle) - im * math.sin(angle)
                if half == 0:
                    out_ref[place, row : row + HALF_TILE, :] = value
                else:
                    out_ref[place, row : row + HALF_TILE, :] += value


def matmul(values, high_ref, low_ref):
    high = values.astype(jnp.bfloat16)
    low = (values - high.astype(jnp.float32)).astype(jnp.bfloat16)
    dot = functools.partial(jnp.dot, preferred_element_type=jnp.float32)
    return dot(high, high_ref[...]) + dot(low, high_ref[...]) + dot(high, low_ref[...])


def spectrum_kernel(taps_ref, ahead_high, ahead_low, twiddle_ref, spec_ref, work_ref, *, outer):
    count = outer // 2

    def load(n, row):
        return taps_ref[row : row + HALF_TILE, n * LANES : (n + 1) * LANES]

    def store(at, row, re, im):
        rows = pl.ds(at * TILE + row, HALF_TILE)
        work_ref[rows, 0:LANES] = re
        work_ref[rows, LANES : 2 * LANES] = im

    for half in range(2):
        outer_forward(load, store, twiddle_ref, outer, half)
    for half in range(2):
        rows = pl.ds(half * count * TILE, count * TILE)
        spec_ref[0, rows, :] = matmul(work_ref[rows, :], ahead_high, ahead_low)


def correlate(piece_refs, me, mate_ref, keep_ref, signal_is_grad, tables, fill_ref, work_ref, out_ref, outer):
    ahead_high, ahead_low, back_high, back_low, twiddle_ref = tables
    count = outer // 2
    per_piece = outer // len(piece_refs)
    for k, ref in enumerate(piece_refs):
        first = (me ^ k) * per_piece
        for i in range(per_piece):
            fill_ref[first + i] = ref[:, i * LANES : (i + 1) * LANES].astype(jnp.float32)

    def load(n, row):
        return fill_ref[n, row : row + HALF_TILE, :]

    def store(at, row, re, im):
        rows = pl.ds(at * TILE + row, HALF_TILE)
        work_ref[rows, 0:LANES] = re
        work_ref[rows, LANES : 2 * LANES] = im

    for half in range(2):
        outer_forward(load, store, twiddle_ref, outer, half)
    for half in range(2):
        rows = pl.ds(half * count * TILE, count * TILE)
        own = matmul(work_ref[rows, :], ahead_high, ahead_low)
        if keep_ref is not None:
            keep_ref[0, rows, :] = own
        mate = mate_ref[0, rows, :]
        grad, other = (own, mate) if signal_is_grad else (mate, own)
        grad_re, grad_im = grad[:, :LANES], grad[:, LANES:]
        other_re, other_im = other[:, :LANES], other[:, LANES:]
        both = jnp.concatenate(
            [other_re * grad_re + other_im * grad_im, other_re * grad_im - other_im * grad_re], axis=1
        )
        work_ref[rows, :] = matmul(both, back_high, back_low)
    for half in range(2):
        outer_inverse(work_ref, twiddle_ref, out_ref, outer, half)


def input_kernel(me_ref, *refs, outer, parts):
    pieces, (mate_ref, *tables) = refs[:parts], refs[parts : parts + 6]
    keep_ref, *sends = refs[parts + 6 : 2 * parts + 7]
    fill_ref, work_ref, out_ref = refs[2 * parts + 7 :]
    me = me_ref[0]
    correlate(pieces, me, mate_ref, keep_ref, True, tables, fill_ref, work_ref, out_ref, outer)
    per_piece = outer // parts
    for k, ref in enumerate(sends):
        first = (me ^ k) * per_piece
        for i in range(per_piece):
            ref[:, i * LANES : (i + 1) * LANES] = out_ref[first + i].astype(jnp.bfloat16)


def filter_kernel(me_ref, *refs, outer, parts):
    pieces, (mate_ref, *tables) = refs[:parts], refs[parts : parts + 6]
    result_ref, fill_ref, work_ref, out_ref = refs[parts + 6 :]
    correlate(pieces, me_ref[0], mate_ref, None, False, tables, fill_ref, work_ref, out_ref, outer)
    for n in range(outer):
        result_ref[:, n * LANES : (n + 1) * LANES] = out_ref[n]


def gather_kernel(me_ref, *refs, pencil):
    *pieces, out_ref, sems = refs
    copies = []
    for k, ref in enumerate(pieces):
        rows = pl.ds((me_ref[0] ^ k) * pencil, pencil)
        copies.append(pltpu.make_async_copy(ref, out_ref.at[rows, :], sems.at[k]))
    for copy in copies:
        copy.start()
    for copy in copies:
        copy.wait()


def shards(layer_input, grad_output, filter_taps):
    parts = lax.axis_size("ctx")
    me = lax.axis_index("ctx")
    pencil, piece = layer_input.shape[0] // parts, layer_input.shape[1]
    length = piece * parts
    outer = length // LANES
    aligned = pencil % TILE == 0
    rows = -(-pencil // TILE) * TILE
    steps = rows // TILE
    ahead, back, back_scaled, twiddle = dft_tables(length)
    me_array = me.astype(jnp.int32).reshape(1)

    def swap(block, k):
        return lax.ppermute(block, "ctx", [(i, i ^ k) for i in range(parts)])

    def pick(array, k):
        blocks = array.reshape(parts, pencil, piece)
        return lax.dynamic_index_in_dim(blocks, me ^ k, 0, keepdims=False)

    def pad(block):
        return block if aligned else jnp.pad(block, ((0, rows - pencil), (0, 0)))

    whole = lambda array: pl.BlockSpec(array.shape, lambda s, *_: (0,) * array.ndim)
    piece_spec = pl.BlockSpec((TILE, piece), lambda s, *_: (s, 0))
    own_spec = pl.BlockSpec((TILE, piece), lambda s, at: (at[0] * steps + s, 0)) if aligned else piece_spec
    full_spec = pl.BlockSpec((TILE, length), lambda s, *_: (s, 0))
    spec_spec = pl.BlockSpec((1, outer * TILE, 2 * LANES), lambda s, *_: (s, 0, 0))
    spec_shape = jax.ShapeDtypeStruct((steps, outer * TILE, 2 * LANES), jnp.float32)
    work = pltpu.VMEM((outer * TILE, 2 * LANES), jnp.float32)
    lane_tiles = pltpu.VMEM((outer, TILE, LANES), jnp.float32)
    params = pltpu.CompilerParams(vmem_limit_bytes=32 * 1024 * 1024)
    stage_flops = 2 * 3 * rows * outer * (2 * LANES) ** 2
    spec_bytes = 4 * rows * length * 2

    def cost(stages, moved):
        return pl.CostEstimate(flops=stages * stage_flops, bytes_accessed=moved, transcendentals=0)

    def own_of(array):
        return array if aligned else pad(pick(array, 0))

    grad_pieces = [swap(pick(grad_output, k), k) for k in range(1, parts)]
    input_pieces = [swap(pick(layer_input, k), k) for k in range(1, parts)]

    taps = pad(filter_taps.reshape(pencil, length))
    taps_spectrum = pl.pallas_call(
        functools.partial(spectrum_kernel, outer=outer),
        grid=(steps,),
        in_specs=[full_spec, whole(ahead[0]), whole(ahead[1]), whole(twiddle)],
        out_specs=spec_spec,
        out_shape=spec_shape,
        scratch_shapes=[work],
        compiler_params=params,
        cost_estimate=cost(1, 2 * spec_bytes),
        name="taps_spectrum",
    )(taps, *ahead, twiddle)

    tables = [*ahead, *back, twiddle]
    grad_spectrum, *outgoing = pl.pallas_call(
        functools.partial(input_kernel, outer=outer, parts=parts),
        grid_spec=pltpu.PrefetchScalarGridSpec(
            num_scalar_prefetch=1,
            grid=(steps,),
            in_specs=[own_spec, *[piece_spec] * (parts - 1), spec_spec, *map(whole, tables)],
            out_specs=[spec_spec, *[piece_spec] * parts],
            scratch_shapes=[lane_tiles, work, lane_tiles],
        ),
        out_shape=[spec_shape, *[jax.ShapeDtypeStruct((rows, piece), jnp.bfloat16)] * parts],
        compiler_params=params,
        cost_estimate=cost(2, 2 * spec_bytes),
        name="grad_input",
    )(me_array, own_of(grad_output), *map(pad, grad_pieces), taps_spectrum, *tables)

    incoming = [outgoing[0][:pencil]] + [swap(outgoing[k][:pencil], k) for k in range(1, parts)]

    tables = [*ahead, *back_scaled, twiddle]
    grad_filter = pl.pallas_call(
        functools.partial(filter_kernel, outer=outer, parts=parts),
        grid_spec=pltpu.PrefetchScalarGridSpec(
            num_scalar_prefetch=1,
            grid=(steps,),
            in_specs=[own_spec, *[piece_spec] * (parts - 1), spec_spec, *map(whole, tables)],
            out_specs=full_spec,
            scratch_shapes=[lane_tiles, work, lane_tiles],
        ),
        out_shape=jax.ShapeDtypeStruct((rows, length), jnp.float32),
        compiler_params=params,
        cost_estimate=cost(2, 2 * spec_bytes),
        name="grad_filter",
    )(me_array, own_of(layer_input), *map(pad, input_pieces), grad_spectrum, *tables)

    if aligned:
        grad_input = pl.pallas_call(
            functools.partial(gather_kernel, pencil=pencil),
            in_specs=[pl.BlockSpec(memory_space=pltpu.SMEM), *[pl.BlockSpec(memory_space=pltpu.VMEM)] * parts],
            out_specs=pl.BlockSpec(memory_space=pl.ANY),
            out_shape=jax.ShapeDtypeStruct((parts * pencil, piece), jnp.bfloat16),
            scratch_shapes=[pltpu.SemaphoreType.DMA((parts,))],
            name="gather_pieces",
        )(me_array, *incoming)
    else:
        slots = jnp.zeros((parts, pencil, piece), jnp.bfloat16)
        for k, block in enumerate(incoming):
            slots = lax.dynamic_update_index_in_dim(slots, block, me ^ k, 0)
        grad_input = slots.reshape(parts * pencil, piece)
    return (grad_input, grad_filter[:pencil].reshape(1, pencil, length))


def solution(mesh):
    in_specs = (P(("dp", "chan"), "ctx"), P(("dp", "chan"), "ctx"), P(("dp", "chan"), "ctx", None))
    out_specs = (P(("dp", "chan"), "ctx"), P(("dp", "chan"), "ctx", None))
    return jax.shard_map(shards, mesh=mesh, in_specs=in_specs, out_specs=out_specs, check_vma=False)
```

```python
import functools
import math

import jax
import jax.numpy as jnp
import ml_dtypes
import numpy as np
from jax import lax
from jax.experimental import pallas as pl
from jax.experimental.pallas import tpu as pltpu
from jax.sharding import PartitionSpec as P

LANES = 128
TILE = 16
HALF_TILE = 8


def split_table(table):
    high = table.astype(ml_dtypes.bfloat16)
    low = (table - high.astype(np.float64)).astype(ml_dtypes.bfloat16)
    return high, low


def dft_tables(length):
    index = np.arange(LANES)
    angle = 2.0 * np.pi * (np.outer(index, index) % LANES) / LANES
    cos, sin = np.cos(angle), np.sin(angle)
    ahead = np.block([[cos, -sin], [sin, cos]])
    back = np.block([[cos, sin], [-sin, cos]]) / length
    outer = length // LANES
    order = np.concatenate([np.arange(0, outer, 2), np.arange(1, outer, 2)])
    turn = 2.0 * np.pi * np.outer(order + 0.25, index) / length
    twiddle = np.stack([np.cos(turn), np.sin(turn)], axis=1).astype(np.float32)
    return split_table(ahead), split_table(back), split_table(back / math.sqrt(length)), twiddle


def add(a, b):
    return (a[0] + b[0], a[1] + b[1])


def sub(a, b):
    return (a[0] - b[0], a[1] - b[1])


def turn_quarter(a, sign):
    return (-a[1], a[0]) if sign > 0 else (a[1], -a[0])


def turn_by(a, numerator, denominator, sign):
    numerator = numerator % denominator
    if numerator == 0:
        return a
    if 4 * numerator == denominator:
        return turn_quarter(a, sign)
    if 2 * numerator == denominator:
        return (-a[0], -a[1])
    if 4 * numerator == 3 * denominator:
        return turn_quarter(a, -sign)
    angle = sign * 2.0 * math.pi * numerator / denominator
    cos, sin = math.cos(angle), math.sin(angle)
    if 8 * numerator % denominator == 0:
        root = math.sqrt(0.5)
        re, im = a
        if cos * sin > 0:
            re, im = re - im, re + im
        else:
            re, im = re + im, im - re
        return (re * (root if cos > 0 else -root), im * (root if cos > 0 else -root))
    return (a[0] * cos - a[1] * sin, a[0] * sin + a[1] * cos)


def fft(points, sign):
    count = len(points)
    if count == 1:
        return points
    if count == 2:
        return [add(points[0], points[1]), sub(points[0], points[1])]
    if count % 4:
        evens, odds = fft(points[0::2], sign), fft(points[1::2], sign)
        turned = [turn_by(odds[k], k, count, sign) for k in range(count // 2)]
        return [add(a, b) for a, b in zip(evens, turned)] + [sub(a, b) for a, b in zip(evens, turned)]
    quarter = count // 4
    parts = [fft(points[r::4], sign) for r in range(4)]
    out = [None] * count
    for k in range(quarter):
        p0, p1, p2, p3 = (turn_by(parts[r][k], r * k, count, sign) for r in range(4))
        s02, d02, s13, d13 = add(p0, p2), sub(p0, p2), add(p1, p3), sub(p1, p3)
        out[k] = add(s02, s13)
        out[k + 2 * quarter] = sub(s02, s13)
        if sign > 0:
            out[k + quarter] = (d02[0] - d13[1], d02[1] + d13[0])
            out[k + 3 * quarter] = (d02[0] + d13[1], d02[1] - d13[0])
        else:
            out[k + quarter] = (d02[0] + d13[1], d02[1] - d13[0])
            out[k + 3 * quarter] = (d02[0] - d13[1], d02[1] + d13[0])
    return out


def outer_forward(load, store, twiddle_ref, outer, half):
    count = outer // 2
    for row in range(0, TILE, HALF_TILE):
        points = []
        for n in range(count):
            near = -2.0 * math.pi * n * (half + 0.25) / outer
            far = -2.0 * math.pi * (n + count) * (half + 0.25) / outer
            a, b = load(n, row), load(n + count, row)
            if n == 0:
                points.append((a + b * math.cos(far), b * math.sin(far)))
            else:
                points.append((a * math.cos(near) + b * math.cos(far), a * math.sin(near) + b * math.sin(far)))
        for k, (re, im) in enumerate(fft(points, -1)):
            at = half * count + k
            cos, sin = twiddle_ref[at, 0:1, :], twiddle_ref[at, 1:2, :]
            store(at, row, re * cos + im * sin, im * cos - re * sin)


def outer_inverse(spec_ref, twiddle_ref, out_ref, outer, half):
    count = outer // 2
    for row in range(0, TILE, HALF_TILE):
        points = []
        for k in range(count):
            at = half * count + k
            rows = pl.ds(at * TILE + row, HALF_TILE)
            re, im = spec_ref[rows, 0:LANES], spec_ref[rows, LANES : 2 * LANES]
            cos, sin = twiddle_ref[at, 0:1, :], twiddle_ref[at, 1:2, :]
            points.append((re * cos - im * sin, re * sin + im * cos))
        for n, (re, im) in enumerate(fft(points, 1)):
            for place in (n, n + count):
                angle = 2.0 * math.pi * place * (half + 0.25) / outer
                value = re if place == 0 else re * math.cos(angle) - im * math.sin(angle)
                if half == 0:
                    out_ref[place, row : row + HALF_TILE, :] = value
                else:
                    out_ref[place, row : row + HALF_TILE, :] += value


def matmul(values, high_ref, low_ref):
    high = values.astype(jnp.bfloat16)
    low = (values - high.astype(jnp.float32)).astype(jnp.bfloat16)
    dot = functools.partial(jnp.dot, preferred_element_type=jnp.float32)
    return dot(high, high_ref[...]) + dot(low, high_ref[...]) + dot(high, low_ref[...])


def put(work_ref, at, row, re, im):
    rows = pl.ds(at * TILE + row, HALF_TILE)
    work_ref[rows, 0:LANES] = re
    work_ref[rows, LANES : 2 * LANES] = im


def spectrum_kernel(me_ref, taps_ref, ahead_high, ahead_low, twiddle_ref, *refs, outer, parts, pencil):
    *moved, spec_ref = refs[:-6]
    taps_here, high_here, low_here, twiddle_here, work_ref, sems = refs[-6:]
    count = outer // 2
    steps = taps_ref.shape[0] // TILE

    def fetch(step):
        rows = pl.ds(step * TILE, TILE)
        return pltpu.make_async_copy(taps_ref.at[rows, :], taps_here.at[rows, :], sems.at[step])

    copies = [
        pltpu.make_async_copy(ahead_high, high_here, sems.at[steps]),
        pltpu.make_async_copy(ahead_low, low_here, sems.at[steps + 1]),
        pltpu.make_async_copy(twiddle_ref, twiddle_here, sems.at[steps + 2]),
    ]
    later = []
    if moved:
        input_ref, grad_ref, *slices, own_grad = moved
        moves = [(input_ref, k, ref) for k, ref in enumerate(slices)] + [(grad_ref, 0, own_grad)]
        for at, (source, k, ref) in enumerate(moves):
            rows = pl.ds((me_ref[0] ^ k) * pencil, pencil)
            later.append(pltpu.make_async_copy(source.at[rows, :], ref, sems.at[steps + 3 + at]))
    fetch(0).start()
    for copy in reversed(copies):
        copy.start()
    for step in range(1, steps):
        fetch(step).start()
    for copy in later:
        copy.start()
    for copy in copies:
        copy.wait()

    @pl.loop(0, steps)
    def _(step):
        fetch(step).wait()

        def load(n, row):
            return taps_here[pl.ds(pl.multiple_of(step * TILE + row, HALF_TILE), HALF_TILE), n * LANES : (n + 1) * LANES]

        for half in range(2):
            outer_forward(load, functools.partial(put, work_ref), twiddle_here, outer, half)
        for half in range(2):
            rows = pl.ds(half * count * TILE, count * TILE)
            spec_ref[step, rows, :] = matmul(work_ref[rows, :], high_here, low_here)

    for copy in later:
        copy.wait()


def correlate(step, piece_refs, me, mate_ref, keep_ref, signal_is_grad, tables, fill_ref, work_ref, out_ref, outer):
    ahead_high, ahead_low, back_high, back_low, twiddle_ref = tables
    count = outer // 2
    per_piece = outer // len(piece_refs)
    rows = pl.ds(pl.multiple_of(step * TILE, TILE), TILE)
    for k, ref in enumerate(piece_refs):
        first = (me ^ k) * per_piece
        for i in range(per_piece):
            fill_ref[first + i] = ref[rows, i * LANES : (i + 1) * LANES].astype(jnp.float32)

    def load(n, row):
        return fill_ref[n, row : row + HALF_TILE, :]

    for half in range(2):
        outer_forward(load, functools.partial(put, work_ref), twiddle_ref, outer, half)
    for half in range(2):
        rows = pl.ds(half * count * TILE, count * TILE)
        own = matmul(work_ref[rows, :], ahead_high, ahead_low)
        if keep_ref is not None:
            keep_ref[step, rows, :] = own
        mate = mate_ref[step, rows, :]
        grad, other = (own, mate) if signal_is_grad else (mate, own)
        grad_re, grad_im = grad[:, :LANES], grad[:, LANES:]
        other_re, other_im = other[:, :LANES], other[:, LANES:]
        both = jnp.concatenate(
            [other_re * grad_re + other_im * grad_im, other_re * grad_im - other_im * grad_re], axis=1
        )
        work_ref[rows, :] = matmul(both, back_high, back_low)
    for half in range(2):
        outer_inverse(work_ref, twiddle_ref, out_ref, outer, half)


def input_kernel(me_ref, *refs, outer, parts):
    pieces, (mate_ref, *tables) = refs[:parts], refs[parts : parts + 6]
    keep_ref, *sends = refs[parts + 6 : 2 * parts + 7]
    fill_ref, work_ref, out_ref = refs[2 * parts + 7 :]
    me = me_ref[0]
    per_piece = outer // parts

    @pl.loop(0, pieces[0].shape[0] // TILE)
    def _(step):
        correlate(step, pieces, me, mate_ref, keep_ref, True, tables, fill_ref, work_ref, out_ref, outer)
        rows = pl.ds(pl.multiple_of(step * TILE, TILE), TILE)
        for k, ref in enumerate(sends):
            first = (me ^ k) * per_piece
            for i in range(per_piece):
                ref[rows, i * LANES : (i + 1) * LANES] = out_ref[first + i].astype(jnp.bfloat16)


def filter_kernel(me_ref, *refs, outer, parts):
    pieces, (mate_ref, *tables) = refs[:parts], refs[parts : parts + 6]
    result_ref, fill_ref, work_ref, out_ref, result_here, sems = refs[parts + 6 :]
    steps = pieces[0].shape[0] // TILE

    def flush(step):
        rows = pl.ds(pl.multiple_of(step * TILE, TILE), TILE)
        return pltpu.make_async_copy(result_here.at[rows, :], result_ref.at[rows, :], sems.at[step])

    @pl.loop(0, steps)
    def _(step):
        correlate(step, pieces, me_ref[0], mate_ref, None, False, tables, fill_ref, work_ref, out_ref, outer)
        rows = pl.ds(pl.multiple_of(step * TILE, TILE), TILE)
        for n in range(outer):
            result_here[rows, n * LANES : (n + 1) * LANES] = out_ref[n]
        flush(step).start()

    @pl.loop(0, steps)
    def _(step):
        flush(step).wait()


def gather_kernel(*refs, pencil):
    *pieces, out_ref, sems = refs
    me = lax.axis_index("ctx")
    copies = []
    for k, ref in enumerate(pieces):
        rows = pl.ds((me ^ k) * pencil, pencil)
        copies.append(pltpu.make_async_copy(ref, out_ref.at[rows, :], sems.at[k]))
    for copy in copies:
        copy.start()
    for copy in copies:
        copy.wait()


def shards(layer_input, grad_output, filter_taps):
    parts = lax.axis_size("ctx")
    me = lax.axis_index("ctx")
    pencil, piece = layer_input.shape[0] // parts, layer_input.shape[1]
    length = piece * parts
    outer = length // LANES
    aligned = pencil % TILE == 0
    rows = -(-pencil // TILE) * TILE
    steps = rows // TILE
    ahead, back, back_scaled, twiddle = dft_tables(length)
    me_array = me.astype(jnp.int32).reshape(1)
    others = sorted(range(1, parts), reverse=True)

    def swap(block, k):
        return lax.ppermute(block, "ctx", [(i, i ^ k) for i in range(parts)])

    def pick(array, k):
        blocks = array.reshape(parts, pencil, piece)
        return lax.dynamic_index_in_dim(blocks, me ^ k, 0, keepdims=False)

    def pad(block):
        return block if aligned else jnp.pad(block, ((0, rows - pencil), (0, 0)))

    scalar = pl.BlockSpec(memory_space=pltpu.SMEM)
    here = pl.BlockSpec(memory_space=pltpu.VMEM)
    there = pl.BlockSpec(memory_space=pl.ANY)
    spec_shape = jax.ShapeDtypeStruct((steps, outer * TILE, 2 * LANES), jnp.float32)
    slice_shape = jax.ShapeDtypeStruct((rows, piece), jnp.bfloat16)
    work = pltpu.VMEM((outer * TILE, 2 * LANES), jnp.float32)
    lane_tiles = pltpu.VMEM((outer, TILE, LANES), jnp.float32)
    params = pltpu.CompilerParams(vmem_limit_bytes=16 * 1024 * 1024)
    stage_flops = 2 * 3 * rows * outer * (2 * LANES) ** 2
    spec_bytes = 4 * rows * length * 2

    def cost(stages, moved):
        return pl.CostEstimate(flops=stages * stage_flops, bytes_accessed=moved, transcendentals=0)

    def in_hbm(array):
        return pltpu.with_memory_space_constraint(array, pltpu.HBM)

    grad_pieces = [None] * parts
    for k in others:
        grad_pieces[k] = swap(pick(grad_output, k), k)

    taps = filter_taps.reshape(pencil, length)
    tables = [*ahead, twiddle]
    slices = parts + 1 if aligned else 0
    results = pl.pallas_call(
        functools.partial(spectrum_kernel, outer=outer, parts=parts, pencil=pencil),
        in_specs=[scalar] + [there] * (6 if aligned else 4),
        out_specs=[here] * (slices + 1),
        out_shape=[slice_shape] * slices + [spec_shape],
        scratch_shapes=[
            pltpu.VMEM((rows, length), jnp.float32),
            *[pltpu.VMEM(table.shape, table.dtype) for table in tables],
            work,
            pltpu.SemaphoreType.DMA((steps + 3 + slices,)),
        ],
        compiler_params=params,
        cost_estimate=cost(1, 2 * spec_bytes),
        name="taps_spectrum",
    )(me_array, in_hbm(pad(taps)), *map(in_hbm, map(jnp.asarray, tables)), *map(in_hbm, [layer_input, grad_output] if aligned else []))
    taps_spectrum = results[-1]
    blocks = results[:parts] if aligned else [pick(layer_input, k) for k in range(parts)]
    grad_pieces[0] = results[parts] if aligned else pick(grad_output, 0)
    input_pieces = [blocks[0]] + [None] * (parts - 1)
    for k in others:
        input_pieces[k] = swap(blocks[k], k)

    tables = [*ahead, *back, twiddle]
    grad_spectrum, *outgoing = pl.pallas_call(
        functools.partial(input_kernel, outer=outer, parts=parts),
        in_specs=[scalar] + [here] * (parts + 1 + len(tables)),
        out_specs=[here] * (parts + 1),
        out_shape=[spec_shape, *[slice_shape] * parts],
        scratch_shapes=[lane_tiles, work, lane_tiles],
        compiler_params=params,
        cost_estimate=cost(2, 2 * spec_bytes),
        name="grad_input",
    )(me_array, *map(pad, grad_pieces), taps_spectrum, *tables)

    incoming = [outgoing[0][:pencil]] + [None] * (parts - 1)
    for k in others:
        incoming[k] = swap(outgoing[k][:pencil], k)

    tables = [*ahead, *back_scaled, twiddle]
    grad_filter = pl.pallas_call(
        functools.partial(filter_kernel, outer=outer, parts=parts),
        in_specs=[scalar] + [here] * (parts + 1 + len(tables)),
        out_specs=there,
        out_shape=jax.ShapeDtypeStruct((rows, length), jnp.float32),
        scratch_shapes=[
            lane_tiles,
            work,
            lane_tiles,
            pltpu.VMEM((rows, length), jnp.float32),
            pltpu.SemaphoreType.DMA((steps,)),
        ],
        compiler_params=params,
        cost_estimate=cost(2, 2 * spec_bytes),
        name="grad_filter",
    )(me_array, *map(pad, input_pieces), grad_spectrum, *tables)

    if aligned:
        grad_input = pl.pallas_call(
            functools.partial(gather_kernel, pencil=pencil),
            in_specs=[there] * parts,
            out_specs=there,
            out_shape=jax.ShapeDtypeStruct((parts * pencil, piece), jnp.bfloat16),
            scratch_shapes=[pltpu.SemaphoreType.DMA((parts,))],
            name="gather_pieces",
        )(*[pltpu.with_memory_space_constraint(block, pltpu.VMEM) for block in incoming])
    else:
        slots = jnp.zeros((parts, pencil, piece), jnp.bfloat16)
        for k, block in enumerate(incoming):
            slots = lax.dynamic_update_index_in_dim(slots, block, me ^ k, 0)
        grad_input = slots.reshape(parts * pencil, piece)
    return (grad_input, grad_filter[:pencil].reshape(1, pencil, length))


def solution(mesh):
    in_specs = (P(("dp", "chan"), "ctx"), P(("dp", "chan"), "ctx"), P(("dp", "chan"), "ctx", None))
    out_specs = (P(("dp", "chan"), "ctx"), P(("dp", "chan"), "ctx", None))
    return jax.shard_map(shards, mesh=mesh, in_specs=in_specs, out_specs=out_specs, check_vma=False)
```

```python
import functools
import math

import jax
import jax.numpy as jnp
import ml_dtypes
import numpy as np
from jax import lax
from jax.experimental import pallas as pl
from jax.experimental.pallas import tpu as pltpu
from jax.sharding import PartitionSpec as P

LANES = 128
TILE = 16
HALF_TILE = 8


def split_table(table):
    high = table.astype(ml_dtypes.bfloat16)
    low = (table - high.astype(np.float64)).astype(ml_dtypes.bfloat16)
    return high, low


def dft_tables(length):
    index = np.arange(LANES)
    angle = 2.0 * np.pi * (np.outer(index, index) % LANES) / LANES
    cos, sin = np.cos(angle), np.sin(angle)
    ahead = np.block([[cos, -sin], [sin, cos]])
    back = np.block([[cos, sin], [-sin, cos]]) / length
    outer = length // LANES
    order = np.concatenate([np.arange(0, outer, 2), np.arange(1, outer, 2)])
    turn = 2.0 * np.pi * np.outer(order + 0.25, index) / length
    twiddle = np.stack([np.cos(turn), np.sin(turn)], axis=1).astype(np.float32)
    return split_table(ahead), split_table(back), split_table(back / math.sqrt(length)), twiddle


def add(a, b):
    return (a[0] + b[0], a[1] + b[1])


def sub(a, b):
    return (a[0] - b[0], a[1] - b[1])


def turn_quarter(a, sign):
    return (-a[1], a[0]) if sign > 0 else (a[1], -a[0])


def turn_by(a, numerator, denominator, sign):
    numerator = numerator % denominator
    if numerator == 0:
        return a
    if 4 * numerator == denominator:
        return turn_quarter(a, sign)
    if 2 * numerator == denominator:
        return (-a[0], -a[1])
    if 4 * numerator == 3 * denominator:
        return turn_quarter(a, -sign)
    angle = sign * 2.0 * math.pi * numerator / denominator
    cos, sin = math.cos(angle), math.sin(angle)
    if 8 * numerator % denominator == 0:
        root = math.sqrt(0.5)
        re, im = a
        if cos * sin > 0:
            re, im = re - im, re + im
        else:
            re, im = re + im, im - re
        return (re * (root if cos > 0 else -root), im * (root if cos > 0 else -root))
    return (a[0] * cos - a[1] * sin, a[0] * sin + a[1] * cos)


def fft(points, sign):
    count = len(points)
    if count == 1:
        return points
    if count == 2:
        return [add(points[0], points[1]), sub(points[0], points[1])]
    if count % 4:
        evens, odds = fft(points[0::2], sign), fft(points[1::2], sign)
        turned = [turn_by(odds[k], k, count, sign) for k in range(count // 2)]
        return [add(a, b) for a, b in zip(evens, turned)] + [sub(a, b) for a, b in zip(evens, turned)]
    quarter = count // 4
    parts = [fft(points[r::4], sign) for r in range(4)]
    out = [None] * count
    for k in range(quarter):
        p0, p1, p2, p3 = (turn_by(parts[r][k], r * k, count, sign) for r in range(4))
        s02, d02, s13, d13 = add(p0, p2), sub(p0, p2), add(p1, p3), sub(p1, p3)
        out[k] = add(s02, s13)
        out[k + 2 * quarter] = sub(s02, s13)
        if sign > 0:
            out[k + quarter] = (d02[0] - d13[1], d02[1] + d13[0])
            out[k + 3 * quarter] = (d02[0] + d13[1], d02[1] - d13[0])
        else:
            out[k + quarter] = (d02[0] + d13[1], d02[1] - d13[0])
            out[k + 3 * quarter] = (d02[0] - d13[1], d02[1] + d13[0])
    return out


def outer_forward(load, store, twiddle_ref, outer, half):
    count = outer // 2
    for row in range(0, TILE, HALF_TILE):
        points = []
        for n in range(count):
            near = -2.0 * math.pi * n * (half + 0.25) / outer
            far = -2.0 * math.pi * (n + count) * (half + 0.25) / outer
            a, b = load(n, row), load(n + count, row)
            if n == 0:
                points.append((a + b * math.cos(far), b * math.sin(far)))
            else:
                points.append((a * math.cos(near) + b * math.cos(far), a * math.sin(near) + b * math.sin(far)))
        for k, (re, im) in enumerate(fft(points, -1)):
            at = half * count + k
            cos, sin = twiddle_ref[at, 0:1, :], twiddle_ref[at, 1:2, :]
            store(at, row, re * cos + im * sin, im * cos - re * sin)


def outer_inverse(spec_ref, twiddle_ref, out_ref, outer, half):
    count = outer // 2
    for row in range(0, TILE, HALF_TILE):
        points = []
        for k in range(count):
            at = half * count + k
            rows = pl.ds(at * TILE + row, HALF_TILE)
            re, im = spec_ref[rows, 0:LANES], spec_ref[rows, LANES : 2 * LANES]
            cos, sin = twiddle_ref[at, 0:1, :], twiddle_ref[at, 1:2, :]
            points.append((re * cos - im * sin, re * sin + im * cos))
        for n, (re, im) in enumerate(fft(points, 1)):
            for place in (n, n + count):
                angle = 2.0 * math.pi * place * (half + 0.25) / outer
                value = re if place == 0 else re * math.cos(angle) - im * math.sin(angle)
                if half == 0:
                    out_ref[place, row : row + HALF_TILE, :] = value
                else:
                    out_ref[place, row : row + HALF_TILE, :] += value


def matmul(values, high_ref, low_ref):
    high = values.astype(jnp.bfloat16)
    low = (values - high.astype(jnp.float32)).astype(jnp.bfloat16)
    dot = functools.partial(jnp.dot, preferred_element_type=jnp.float32)
    return dot(high, high_ref[...]) + dot(low, high_ref[...]) + dot(high, low_ref[...])


def order_of(what, parts):
    near = list(range(1, parts))
    return {"grad": near[-1:] + near[:-1], "input": near, "back": near[::-1]}[what]


def places_of(what, parts):
    me = lax.axis_index("ctx")
    return [me ^ k for k in [0, *order_of(what, parts)]]


def put(work_ref, at, row, re, im):
    rows = pl.ds(at * TILE + row, HALF_TILE)
    work_ref[rows, 0:LANES] = re
    work_ref[rows, LANES : 2 * LANES] = im


def spectrum_kernel(taps_ref, ahead_high, ahead_low, twiddle_ref, *refs, outer, parts, pencil):
    *moved, spec_ref = refs[:-6]
    taps_here, high_here, low_here, twiddle_here, work_ref, sems = refs[-6:]
    count = outer // 2
    steps = taps_ref.shape[0] // TILE

    def fetch(step):
        rows = pl.ds(step * TILE, TILE)
        return pltpu.make_async_copy(taps_ref.at[rows, :], taps_here.at[rows, :], sems.at[step])

    copies = [
        pltpu.make_async_copy(ahead_high, high_here, sems.at[steps]),
        pltpu.make_async_copy(ahead_low, low_here, sems.at[steps + 1]),
        pltpu.make_async_copy(twiddle_ref, twiddle_here, sems.at[steps + 2]),
    ]
    later = []
    if moved:
        input_ref, grad_ref, *slices, own_grad = moved
        places = places_of("input", parts)
        moves = [(input_ref, *move) for move in zip(places, slices)] + [(grad_ref, places[0], own_grad)]
        for at, (source, place, ref) in enumerate(moves):
            rows = pl.ds(place * pencil, pencil)
            later.append(pltpu.make_async_copy(source.at[rows, :], ref, sems.at[steps + 3 + at]))
    fetch(0).start()
    for copy in reversed(copies):
        copy.start()
    for step in range(1, steps):
        fetch(step).start()
    for copy in later:
        copy.start()
    for copy in copies:
        copy.wait()

    @pl.loop(0, steps)
    def _(step):
        fetch(step).wait()

        def load(n, row):
            return taps_here[pl.ds(pl.multiple_of(step * TILE + row, HALF_TILE), HALF_TILE), n * LANES : (n + 1) * LANES]

        for half in range(2):
            outer_forward(load, functools.partial(put, work_ref), twiddle_here, outer, half)
        for half in range(2):
            rows = pl.ds(half * count * TILE, count * TILE)
            spec_ref[step, rows, :] = matmul(work_ref[rows, :], high_here, low_here)

    for copy in later:
        copy.wait()


def correlate(step, piece_refs, places, mate_ref, keep_ref, signal_is_grad, tables, fill_ref, work_ref, out_ref, outer):
    ahead_high, ahead_low, back_high, back_low, twiddle_ref = tables
    count = outer // 2
    per_piece = outer // len(piece_refs)
    rows = pl.ds(pl.multiple_of(step * TILE, TILE), TILE)
    for place, ref in zip(places, piece_refs):
        first = place * per_piece
        for i in range(per_piece):
            fill_ref[first + i] = ref[rows, i * LANES : (i + 1) * LANES].astype(jnp.float32)

    def load(n, row):
        return fill_ref[n, row : row + HALF_TILE, :]

    for half in range(2):
        outer_forward(load, functools.partial(put, work_ref), twiddle_ref, outer, half)
    for half in range(2):
        rows = pl.ds(half * count * TILE, count * TILE)
        own = matmul(work_ref[rows, :], ahead_high, ahead_low)
        if keep_ref is not None:
            keep_ref[step, rows, :] = own
        mate = mate_ref[step, rows, :]
        grad, other = (own, mate) if signal_is_grad else (mate, own)
        grad_re, grad_im = grad[:, :LANES], grad[:, LANES:]
        other_re, other_im = other[:, :LANES], other[:, LANES:]
        both = jnp.concatenate(
            [other_re * grad_re + other_im * grad_im, other_re * grad_im - other_im * grad_re], axis=1
        )
        work_ref[rows, :] = matmul(both, back_high, back_low)
    for half in range(2):
        outer_inverse(work_ref, twiddle_ref, out_ref, outer, half)


def input_kernel(*refs, outer, parts):
    pieces, (mate_ref, *tables) = refs[:parts], refs[parts : parts + 6]
    keep_ref, *sends = refs[parts + 6 : 2 * parts + 7]
    fill_ref, work_ref, out_ref = refs[2 * parts + 7 :]
    places, send_places = places_of("grad", parts), places_of("back", parts)
    per_piece = outer // parts

    @pl.loop(0, pieces[0].shape[0] // TILE)
    def _(step):
        correlate(step, pieces, places, mate_ref, keep_ref, True, tables, fill_ref, work_ref, out_ref, outer)
        rows = pl.ds(pl.multiple_of(step * TILE, TILE), TILE)
        for place, ref in zip(send_places, sends):
            first = place * per_piece
            for i in range(per_piece):
                ref[rows, i * LANES : (i + 1) * LANES] = out_ref[first + i].astype(jnp.bfloat16)


def filter_kernel(*refs, outer, parts):
    pieces, (mate_ref, *tables) = refs[:parts], refs[parts : parts + 6]
    result_ref, fill_ref, work_ref, out_ref, result_here, sems = refs[parts + 6 :]
    places = places_of("input", parts)
    steps = pieces[0].shape[0] // TILE

    def flush(step):
        rows = pl.ds(pl.multiple_of(step * TILE, TILE), TILE)
        return pltpu.make_async_copy(result_here.at[rows, :], result_ref.at[rows, :], sems.at[step])

    @pl.loop(0, steps)
    def _(step):
        correlate(step, pieces, places, mate_ref, None, False, tables, fill_ref, work_ref, out_ref, outer)
        rows = pl.ds(pl.multiple_of(step * TILE, TILE), TILE)
        for n in range(outer):
            result_here[rows, n * LANES : (n + 1) * LANES] = out_ref[n]
        flush(step).start()

    @pl.loop(0, steps)
    def _(step):
        flush(step).wait()


def slice_kernel(source_ref, *refs, parts, pencil):
    *blocks, sems = refs
    copies = []
    for place, ref in zip(places_of("grad", parts)[2:], blocks):
        rows = pl.ds(place * pencil, pencil)
        copies.append(pltpu.make_async_copy(source_ref.at[rows, :], ref, sems.at[len(copies)]))
    for copy in copies:
        copy.start()
    for copy in copies:
        copy.wait()


def gather_kernel(*refs, pencil):
    *pieces, out_ref, sems = refs
    copies = []
    for place, ref in zip(places_of("back", len(pieces)), pieces):
        rows = pl.ds(place * pencil, pencil)
        copies.append(pltpu.make_async_copy(ref, out_ref.at[rows, :], sems.at[len(copies)]))
    for copy in copies:
        copy.start()
    for copy in copies:
        copy.wait()


def shards(layer_input, grad_output, filter_taps):
    parts = lax.axis_size("ctx")
    pencil, piece = layer_input.shape[0] // parts, layer_input.shape[1]
    length = piece * parts
    outer = length // LANES
    aligned = pencil % TILE == 0
    rows = -(-pencil // TILE) * TILE
    steps = rows // TILE
    ahead, back, back_scaled, twiddle = dft_tables(length)
    def exchange(what, blocks):
        pairs = [[(i, i ^ k) for i in range(parts)] for k in order_of(what, parts)]
        return [lax.ppermute(block, "ctx", pair) for block, pair in zip(blocks, pairs)]

    def pick(array, place):
        blocks = array.reshape(parts, pencil, piece)
        return lax.dynamic_index_in_dim(blocks, place, 0, keepdims=False)

    def pad(block):
        return block if aligned else jnp.pad(block, ((0, rows - pencil), (0, 0)))

    here = pl.BlockSpec(memory_space=pltpu.VMEM)
    there = pl.BlockSpec(memory_space=pl.ANY)
    spec_shape = jax.ShapeDtypeStruct((steps, outer * TILE, 2 * LANES), jnp.float32)
    slice_shape = jax.ShapeDtypeStruct((rows, piece), jnp.bfloat16)
    work = pltpu.VMEM((outer * TILE, 2 * LANES), jnp.float32)
    lane_tiles = pltpu.VMEM((outer, TILE, LANES), jnp.float32)
    params = pltpu.CompilerParams(vmem_limit_bytes=16 * 1024 * 1024)
    stage_flops = 2 * 3 * rows * outer * (2 * LANES) ** 2
    spec_bytes = 4 * rows * length * 2

    def cost(stages, moved):
        return pl.CostEstimate(flops=stages * stage_flops, bytes_accessed=moved, transcendentals=0)

    def in_hbm(array):
        return pltpu.with_memory_space_constraint(array, pltpu.HBM)

    own, *others = places_of("grad", parts)
    if aligned:
        blocks = pl.pallas_call(
            functools.partial(slice_kernel, parts=parts, pencil=pencil),
            in_specs=[there],
            out_specs=[here] * (parts - 2),
            out_shape=[slice_shape] * (parts - 2),
            scratch_shapes=[pltpu.SemaphoreType.DMA((parts - 2,))],
            cost_estimate=cost(0, 2 * (parts - 2) * pencil * piece * 2),
            name="slice_grad",
        )(in_hbm(grad_output))
    else:
        blocks = [pick(grad_output, place) for place in others[1:]]
    grad_pieces = exchange("grad", [pick(grad_output, others[0]), *blocks])

    taps = filter_taps.reshape(pencil, length)
    tables = [*ahead, twiddle]
    slices = parts + 1 if aligned else 0
    results = pl.pallas_call(
        functools.partial(spectrum_kernel, outer=outer, parts=parts, pencil=pencil),
        in_specs=[there] * (6 if aligned else 4),
        out_specs=[here] * (slices + 1),
        out_shape=[slice_shape] * slices + [spec_shape],
        scratch_shapes=[
            pltpu.VMEM((rows, length), jnp.float32),
            *[pltpu.VMEM(table.shape, table.dtype) for table in tables],
            work,
            pltpu.SemaphoreType.DMA((steps + 3 + slices,)),
        ],
        compiler_params=params,
        cost_estimate=cost(1, 2 * spec_bytes),
        name="taps_spectrum",
    )(*map(in_hbm, [pad(taps), *map(jnp.asarray, tables), *([layer_input, grad_output] if aligned else [])]))
    taps_spectrum = results[-1]
    blocks = results[:parts] if aligned else [pick(layer_input, place) for place in places_of("input", parts)]
    grad_pieces = [results[parts] if aligned else pick(grad_output, own), *grad_pieces]
    input_pieces = [blocks[0], *exchange("input", blocks[1:])]

    tables = [*ahead, *back, twiddle]
    grad_spectrum, *outgoing = pl.pallas_call(
        functools.partial(input_kernel, outer=outer, parts=parts),
        in_specs=[here] * (parts + 1 + len(tables)),
        out_specs=[here] * (parts + 1),
        out_shape=[spec_shape, *[slice_shape] * parts],
        scratch_shapes=[lane_tiles, work, lane_tiles],
        compiler_params=params,
        cost_estimate=cost(2, 2 * spec_bytes),
        name="grad_input",
    )(*map(pad, grad_pieces), taps_spectrum, *tables)

    outgoing = [block[:pencil] for block in outgoing]
    incoming = [outgoing[0], *exchange("back", outgoing[1:])]

    tables = [*ahead, *back_scaled, twiddle]
    grad_filter = pl.pallas_call(
        functools.partial(filter_kernel, outer=outer, parts=parts),
        in_specs=[here] * (parts + 1 + len(tables)),
        out_specs=there,
        out_shape=jax.ShapeDtypeStruct((rows, length), jnp.float32),
        scratch_shapes=[
            lane_tiles,
            work,
            lane_tiles,
            pltpu.VMEM((rows, length), jnp.float32),
            pltpu.SemaphoreType.DMA((steps,)),
        ],
        compiler_params=params,
        cost_estimate=cost(2, 2 * spec_bytes),
        name="grad_filter",
    )(*map(pad, input_pieces), grad_spectrum, *tables)

    if aligned:
        grad_input = pl.pallas_call(
            functools.partial(gather_kernel, pencil=pencil),
            in_specs=[there] * parts,
            out_specs=there,
            out_shape=jax.ShapeDtypeStruct((parts * pencil, piece), jnp.bfloat16),
            scratch_shapes=[pltpu.SemaphoreType.DMA((parts,))],
            name="gather_pieces",
        )(*[pltpu.with_memory_space_constraint(block, pltpu.VMEM) for block in incoming])
    else:
        grad_input = jnp.zeros((parts, pencil, piece), jnp.bfloat16)
        for place, block in zip(places_of("back", parts), incoming):
            grad_input = lax.dynamic_update_index_in_dim(grad_input, block, place, 0)
        grad_input = grad_input.reshape(parts * pencil, piece)
    return (grad_input, grad_filter[:pencil].reshape(1, pencil, length))


def solution(mesh):
    in_specs = (P(("dp", "chan"), "ctx"), P(("dp", "chan"), "ctx"), P(("dp", "chan"), "ctx", None))
    out_specs = (P(("dp", "chan"), "ctx"), P(("dp", "chan"), "ctx", None))
    return jax.shard_map(shards, mesh=mesh, in_specs=in_specs, out_specs=out_specs, check_vma=False)
```

```python
import functools
import math

import jax
import jax.numpy as jnp
import ml_dtypes
import numpy as np
from jax import lax
from jax.experimental import pallas as pl
from jax.experimental.pallas import tpu as pltpu
from jax.sharding import PartitionSpec as P

LANES = 128
TILE = 16
HALF_TILE = 8


def split_table(table):
    high = table.astype(ml_dtypes.bfloat16)
    low = (table - high.astype(np.float64)).astype(ml_dtypes.bfloat16)
    return high, low


def dft_tables(length):
    index = np.arange(LANES)
    angle = 2.0 * np.pi * (np.outer(index, index) % LANES) / LANES
    cos, sin = np.cos(angle), np.sin(angle)
    ahead = np.block([[cos, -sin], [sin, cos]])
    back = np.block([[cos, sin], [-sin, cos]]) / length
    outer = length // LANES
    order = np.concatenate([np.arange(0, outer, 2), np.arange(1, outer, 2)])
    turn = 2.0 * np.pi * np.outer(order + 0.25, index) / length
    twiddle = np.stack([np.cos(turn), np.sin(turn)], axis=1).astype(np.float32)
    return split_table(ahead), split_table(back), split_table(back / math.sqrt(length)), twiddle


def add(a, b):
    return (a[0] + b[0], a[1] + b[1])


def sub(a, b):
    return (a[0] - b[0], a[1] - b[1])


def turn_quarter(a, sign):
    return (-a[1], a[0]) if sign > 0 else (a[1], -a[0])


def turn_by(a, numerator, denominator, sign):
    numerator = numerator % denominator
    if numerator == 0:
        return a
    if 4 * numerator == denominator:
        return turn_quarter(a, sign)
    if 2 * numerator == denominator:
        return (-a[0], -a[1])
    if 4 * numerator == 3 * denominator:
        return turn_quarter(a, -sign)
    angle = sign * 2.0 * math.pi * numerator / denominator
    cos, sin = math.cos(angle), math.sin(angle)
    if 8 * numerator % denominator == 0:
        root = math.sqrt(0.5)
        re, im = a
        if cos * sin > 0:
            re, im = re - im, re + im
        else:
            re, im = re + im, im - re
        return (re * (root if cos > 0 else -root), im * (root if cos > 0 else -root))
    return (a[0] * cos - a[1] * sin, a[0] * sin + a[1] * cos)


def fft(points, sign):
    count = len(points)
    if count == 1:
        return points
    if count == 2:
        return [add(points[0], points[1]), sub(points[0], points[1])]
    if count % 4:
        evens, odds = fft(points[0::2], sign), fft(points[1::2], sign)
        turned = [turn_by(odds[k], k, count, sign) for k in range(count // 2)]
        return [add(a, b) for a, b in zip(evens, turned)] + [sub(a, b) for a, b in zip(evens, turned)]
    quarter = count // 4
    parts = [fft(points[r::4], sign) for r in range(4)]
    out = [None] * count
    for k in range(quarter):
        p0, p1, p2, p3 = (turn_by(parts[r][k], r * k, count, sign) for r in range(4))
        s02, d02, s13, d13 = add(p0, p2), sub(p0, p2), add(p1, p3), sub(p1, p3)
        out[k] = add(s02, s13)
        out[k + 2 * quarter] = sub(s02, s13)
        if sign > 0:
            out[k + quarter] = (d02[0] - d13[1], d02[1] + d13[0])
            out[k + 3 * quarter] = (d02[0] + d13[1], d02[1] - d13[0])
        else:
            out[k + quarter] = (d02[0] + d13[1], d02[1] - d13[0])
            out[k + 3 * quarter] = (d02[0] - d13[1], d02[1] + d13[0])
    return out


def outer_forward(load, store, twiddle_ref, outer, half):
    count = outer // 2
    for row in range(0, TILE, HALF_TILE):
        points = []
        for n in range(count):
            near = -2.0 * math.pi * n * (half + 0.25) / outer
            far = -2.0 * math.pi * (n + count) * (half + 0.25) / outer
            a, b = load(n, row), load(n + count, row)
            if n == 0:
                points.append((a + b * math.cos(far), b * math.sin(far)))
            else:
                points.append((a * math.cos(near) + b * math.cos(far), a * math.sin(near) + b * math.sin(far)))
        for k, (re, im) in enumerate(fft(points, -1)):
            at = half * count + k
            cos, sin = twiddle_ref[at, 0:1, :], twiddle_ref[at, 1:2, :]
            store(at, row, re * cos + im * sin, im * cos - re * sin)


def outer_inverse(spec_ref, twiddle_ref, out_ref, outer, half):
    count = outer // 2
    for row in range(0, TILE, HALF_TILE):
        points = []
        for k in range(count):
            at = half * count + k
            rows = pl.ds(at * TILE + row, HALF_TILE)
            re, im = spec_ref[rows, 0:LANES], spec_ref[rows, LANES : 2 * LANES]
            cos, sin = twiddle_ref[at, 0:1, :], twiddle_ref[at, 1:2, :]
            points.append((re * cos - im * sin, re * sin + im * cos))
        for n, (re, im) in enumerate(fft(points, 1)):
            for place in (n, n + count):
                angle = 2.0 * math.pi * place * (half + 0.25) / outer
                value = re if place == 0 else re * math.cos(angle) - im * math.sin(angle)
                if half == 0:
                    out_ref[place, row : row + HALF_TILE, :] = value
                else:
                    out_ref[place, row : row + HALF_TILE, :] += value


def matmul(values, high_ref, low_ref):
    high = values.astype(jnp.bfloat16)
    low = (values - high.astype(jnp.float32)).astype(jnp.bfloat16)
    dot = functools.partial(jnp.dot, preferred_element_type=jnp.float32)
    both = dot(jnp.concatenate([high, low], axis=0), high_ref[...])
    count = high.shape[0]
    return both[:count] + both[count:] + dot(high, low_ref[...])


def order_of(what, parts):
    near = list(range(1, parts))
    return {"grad": near[-1:] + near[:-1], "input": near, "back": near[::-1]}[what]


def places_of(what, parts):
    me = lax.axis_index("ctx")
    return [me ^ k for k in [0, *order_of(what, parts)]]


def put(work_ref, at, row, re, im):
    rows = pl.ds(at * TILE + row, HALF_TILE)
    work_ref[rows, 0:LANES] = re
    work_ref[rows, LANES : 2 * LANES] = im


def spectrum_kernel(taps_ref, ahead_high, ahead_low, twiddle_ref, *refs, outer, parts, pencil):
    *moved, spec_ref = refs[:-6]
    taps_here, high_here, low_here, twiddle_here, work_ref, sems = refs[-6:]
    count = outer // 2
    steps = taps_ref.shape[0] // TILE

    def fetch(step):
        rows = pl.ds(step * TILE, TILE)
        return pltpu.make_async_copy(taps_ref.at[rows, :], taps_here.at[rows, :], sems.at[step])

    copies = [
        pltpu.make_async_copy(ahead_high, high_here, sems.at[steps]),
        pltpu.make_async_copy(ahead_low, low_here, sems.at[steps + 1]),
        pltpu.make_async_copy(twiddle_ref, twiddle_here, sems.at[steps + 2]),
    ]
    later = []
    if moved:
        input_ref, grad_ref, *slices, own_grad = moved
        places = places_of("input", parts)
        moves = [(input_ref, *move) for move in zip(places, slices)] + [(grad_ref, places[0], own_grad)]
        for at, (source, place, ref) in enumerate(moves):
            rows = pl.ds(place * pencil, pencil)
            later.append(pltpu.make_async_copy(source.at[rows, :], ref, sems.at[steps + 3 + at]))
    fetch(0).start()
    for copy in reversed(copies):
        copy.start()
    for step in range(1, steps):
        fetch(step).start()
    for copy in later:
        copy.start()
    for copy in copies:
        copy.wait()

    @pl.loop(0, steps)
    def _(step):
        fetch(step).wait()

        def load(n, row):
            return taps_here[pl.ds(pl.multiple_of(step * TILE + row, HALF_TILE), HALF_TILE), n * LANES : (n + 1) * LANES]

        for half in range(2):
            outer_forward(load, functools.partial(put, work_ref), twiddle_here, outer, half)
        for half in range(2):
            rows = pl.ds(half * count * TILE, count * TILE)
            spec_ref[step, rows, :] = matmul(work_ref[rows, :], high_here, low_here)

    for copy in later:
        copy.wait()


def correlate(step, piece_refs, places, mate_ref, keep_ref, signal_is_grad, tables, fill_ref, work_ref, out_ref, outer):
    ahead_high, ahead_low, back_high, back_low, twiddle_ref = tables
    count = outer // 2
    per_piece = outer // len(piece_refs)
    rows = pl.ds(pl.multiple_of(step * TILE, TILE), TILE)
    for place, ref in zip(places, piece_refs):
        first = place * per_piece
        for i in range(per_piece):
            fill_ref[first + i] = ref[rows, i * LANES : (i + 1) * LANES].astype(jnp.float32)

    def load(n, row):
        return fill_ref[n, row : row + HALF_TILE, :]

    for half in range(2):
        outer_forward(load, functools.partial(put, work_ref), twiddle_ref, outer, half)
    for half in range(2):
        rows = pl.ds(half * count * TILE, count * TILE)
        own = matmul(work_ref[rows, :], ahead_high, ahead_low)
        if keep_ref is not None:
            keep_ref[step, rows, :] = own
        mate = mate_ref[step, rows, :]
        grad, other = (own, mate) if signal_is_grad else (mate, own)
        grad_re, grad_im = grad[:, :LANES], grad[:, LANES:]
        other_re, other_im = other[:, :LANES], other[:, LANES:]
        both = jnp.concatenate(
            [other_re * grad_re + other_im * grad_im, other_re * grad_im - other_im * grad_re], axis=1
        )
        work_ref[rows, :] = matmul(both, back_high, back_low)
    for half in range(2):
        outer_inverse(work_ref, twiddle_ref, out_ref, outer, half)


def input_kernel(*refs, outer, parts):
    pieces, (mate_ref, *tables) = refs[:parts], refs[parts : parts + 6]
    keep_ref, *sends = refs[parts + 6 : 2 * parts + 7]
    fill_ref, work_ref, out_ref = refs[2 * parts + 7 :]
    places, send_places = places_of("grad", parts), places_of("back", parts)
    per_piece = outer // parts

    @pl.loop(0, pieces[0].shape[0] // TILE)
    def _(step):
        correlate(step, pieces, places, mate_ref, keep_ref, True, tables, fill_ref, work_ref, out_ref, outer)
        rows = pl.ds(pl.multiple_of(step * TILE, TILE), TILE)
        for place, ref in zip(send_places, sends):
            first = place * per_piece
            for i in range(per_piece):
                ref[rows, i * LANES : (i + 1) * LANES] = out_ref[first + i].astype(jnp.bfloat16)


def filter_kernel(*refs, outer, parts):
    pieces, (mate_ref, *tables) = refs[:parts], refs[parts : parts + 6]
    result_ref, fill_ref, work_ref, out_ref, result_here, sems = refs[parts + 6 :]
    places = places_of("input", parts)
    steps = pieces[0].shape[0] // TILE

    def flush(step):
        rows = pl.ds(pl.multiple_of(step * TILE, TILE), TILE)
        return pltpu.make_async_copy(result_here.at[rows, :], result_ref.at[rows, :], sems.at[step])

    @pl.loop(0, steps)
    def _(step):
        correlate(step, pieces, places, mate_ref, None, False, tables, fill_ref, work_ref, out_ref, outer)
        rows = pl.ds(pl.multiple_of(step * TILE, TILE), TILE)
        for n in range(outer):
            result_here[rows, n * LANES : (n + 1) * LANES] = out_ref[n]
        flush(step).start()

    @pl.loop(0, steps)
    def _(step):
        flush(step).wait()


def slice_kernel(source_ref, *refs, parts, pencil):
    *blocks, sems = refs
    copies = []
    for place, ref in zip(places_of("grad", parts)[2:], blocks):
        rows = pl.ds(place * pencil, pencil)
        copies.append(pltpu.make_async_copy(source_ref.at[rows, :], ref, sems.at[len(copies)]))
    for copy in copies:
        copy.start()
    for copy in copies:
        copy.wait()


def gather_kernel(*refs, pencil):
    *pieces, out_ref, sems = refs
    copies = []
    for place, ref in zip(places_of("back", len(pieces)), pieces):
        rows = pl.ds(place * pencil, pencil)
        copies.append(pltpu.make_async_copy(ref, out_ref.at[rows, :], sems.at[len(copies)]))
    for copy in copies:
        copy.start()
    for copy in copies:
        copy.wait()


def shards(layer_input, grad_output, filter_taps):
    parts = lax.axis_size("ctx")
    pencil, piece = layer_input.shape[0] // parts, layer_input.shape[1]
    length = piece * parts
    outer = length // LANES
    aligned = pencil % TILE == 0
    rows = -(-pencil // TILE) * TILE
    steps = rows // TILE
    ahead, back, back_scaled, twiddle = dft_tables(length)
    def exchange(what, blocks):
        pairs = [[(i, i ^ k) for i in range(parts)] for k in order_of(what, parts)]
        return [lax.ppermute(block, "ctx", pair) for block, pair in zip(blocks, pairs)]

    def pick(array, place):
        blocks = array.reshape(parts, pencil, piece)
        return lax.dynamic_index_in_dim(blocks, place, 0, keepdims=False)

    def pad(block):
        return block if aligned else jnp.pad(block, ((0, rows - pencil), (0, 0)))

    here = pl.BlockSpec(memory_space=pltpu.VMEM)
    there = pl.BlockSpec(memory_space=pl.ANY)
    spec_shape = jax.ShapeDtypeStruct((steps, outer * TILE, 2 * LANES), jnp.float32)
    slice_shape = jax.ShapeDtypeStruct((rows, piece), jnp.bfloat16)
    work = pltpu.VMEM((outer * TILE, 2 * LANES), jnp.float32)
    lane_tiles = pltpu.VMEM((outer, TILE, LANES), jnp.float32)
    params = pltpu.CompilerParams(vmem_limit_bytes=16 * 1024 * 1024)
    stage_flops = 2 * 3 * rows * outer * (2 * LANES) ** 2
    spec_bytes = 4 * rows * length * 2

    def cost(stages, moved):
        return pl.CostEstimate(flops=stages * stage_flops, bytes_accessed=moved, transcendentals=0)

    def in_hbm(array):
        return pltpu.with_memory_space_constraint(array, pltpu.HBM)

    own, *others = places_of("grad", parts)
    if aligned:
        blocks = pl.pallas_call(
            functools.partial(slice_kernel, parts=parts, pencil=pencil),
            in_specs=[there],
            out_specs=[here] * (parts - 2),
            out_shape=[slice_shape] * (parts - 2),
            scratch_shapes=[pltpu.SemaphoreType.DMA((parts - 2,))],
            cost_estimate=cost(0, 2 * (parts - 2) * pencil * piece * 2),
            name="slice_grad",
        )(in_hbm(grad_output))
    else:
        blocks = [pick(grad_output, place) for place in others[1:]]
    grad_pieces = exchange("grad", [pick(grad_output, others[0]), *blocks])

    taps = filter_taps.reshape(pencil, length)
    tables = [*ahead, twiddle]
    slices = parts + 1 if aligned else 0
    results = pl.pallas_call(
        functools.partial(spectrum_kernel, outer=outer, parts=parts, pencil=pencil),
        in_specs=[there] * (6 if aligned else 4),
        out_specs=[here] * (slices + 1),
        out_shape=[slice_shape] * slices + [spec_shape],
        scratch_shapes=[
            pltpu.VMEM((rows, length), jnp.float32),
            *[pltpu.VMEM(table.shape, table.dtype) for table in tables],
            work,
            pltpu.SemaphoreType.DMA((steps + 3 + slices,)),
        ],
        compiler_params=params,
        cost_estimate=cost(1, 2 * spec_bytes),
        name="taps_spectrum",
    )(*map(in_hbm, [pad(taps), *map(jnp.asarray, tables), *([layer_input, grad_output] if aligned else [])]))
    taps_spectrum = results[-1]
    blocks = results[:parts] if aligned else [pick(layer_input, place) for place in places_of("input", parts)]
    grad_pieces = [results[parts] if aligned else pick(grad_output, own), *grad_pieces]
    input_pieces = [blocks[0], *exchange("input", blocks[1:])]

    tables = [*ahead, *back, twiddle]
    grad_spectrum, *outgoing = pl.pallas_call(
        functools.partial(input_kernel, outer=outer, parts=parts),
        in_specs=[here] * (parts + 1 + len(tables)),
        out_specs=[here] * (parts + 1),
        out_shape=[spec_shape, *[slice_shape] * parts],
        scratch_shapes=[lane_tiles, work, lane_tiles],
        compiler_params=params,
        cost_estimate=cost(2, 2 * spec_bytes),
        name="grad_input",
    )(*map(pad, grad_pieces), taps_spectrum, *tables)

    outgoing = [block[:pencil] for block in outgoing]
    incoming = [outgoing[0], *exchange("back", outgoing[1:])]

    tables = [*ahead, *back_scaled, twiddle]
    grad_filter = pl.pallas_call(
        functools.partial(filter_kernel, outer=outer, parts=parts),
        in_specs=[here] * (parts + 1 + len(tables)),
        out_specs=there,
        out_shape=jax.ShapeDtypeStruct((rows, length), jnp.float32),
        scratch_shapes=[
            lane_tiles,
            work,
            lane_tiles,
            pltpu.VMEM((rows, length), jnp.float32),
            pltpu.SemaphoreType.DMA((steps,)),
        ],
        compiler_params=params,
        cost_estimate=cost(2, 2 * spec_bytes),
        name="grad_filter",
    )(*map(pad, input_pieces), grad_spectrum, *tables)

    if aligned:
        grad_input = pl.pallas_call(
            functools.partial(gather_kernel, pencil=pencil),
            in_specs=[there] * parts,
            out_specs=there,
            out_shape=jax.ShapeDtypeStruct((parts * pencil, piece), jnp.bfloat16),
            scratch_shapes=[pltpu.SemaphoreType.DMA((parts,))],
            name="gather_pieces",
        )(*[pltpu.with_memory_space_constraint(block, pltpu.VMEM) for block in incoming])
    else:
        grad_input = jnp.zeros((parts, pencil, piece), jnp.bfloat16)
        for place, block in zip(places_of("back", parts), incoming):
            grad_input = lax.dynamic_update_index_in_dim(grad_input, block, place, 0)
        grad_input = grad_input.reshape(parts * pencil, piece)
    return (grad_input, grad_filter[:pencil].reshape(1, pencil, length))


def solution(mesh):
    in_specs = (P(("dp", "chan"), "ctx"), P(("dp", "chan"), "ctx"), P(("dp", "chan"), "ctx", None))
    out_specs = (P(("dp", "chan"), "ctx"), P(("dp", "chan"), "ctx", None))
    return jax.shard_map(shards, mesh=mesh, in_specs=in_specs, out_specs=out_specs, check_vma=False)
```

```python
import functools
import math

import jax
import jax.numpy as jnp
import ml_dtypes
import numpy as np
from jax import lax
from jax.experimental import pallas as pl
from jax.experimental.pallas import tpu as pltpu
from jax.sharding import PartitionSpec as P

LANES = 128
TILE = 16
HALF_TILE = 8


def split_table(table):
    high = table.astype(ml_dtypes.bfloat16)
    low = (table - high.astype(np.float64)).astype(ml_dtypes.bfloat16)
    return high, low


def dft_tables(length):
    index = np.arange(LANES)
    angle = 2.0 * np.pi * (np.outer(index, index) % LANES) / LANES
    cos, sin = np.cos(angle), np.sin(angle)
    ahead = np.block([[cos, -sin], [sin, cos]])
    back = np.block([[cos, sin], [-sin, cos]]) / length
    outer = length // LANES
    order = np.concatenate([np.arange(0, outer, 2), np.arange(1, outer, 2)])
    turn = 2.0 * np.pi * np.outer(order + 0.25, index) / length
    twiddle = np.stack([np.cos(turn), np.sin(turn)], axis=1).astype(np.float32)
    return split_table(ahead), split_table(back), split_table(back / math.sqrt(length)), twiddle


def add(a, b):
    return (a[0] + b[0], a[1] + b[1])


def sub(a, b):
    return (a[0] - b[0], a[1] - b[1])


def turn_quarter(a, sign):
    return (-a[1], a[0]) if sign > 0 else (a[1], -a[0])


def turn_by(a, numerator, denominator, sign):
    numerator = numerator % denominator
    if numerator == 0:
        return a
    if 4 * numerator == denominator:
        return turn_quarter(a, sign)
    if 2 * numerator == denominator:
        return (-a[0], -a[1])
    if 4 * numerator == 3 * denominator:
        return turn_quarter(a, -sign)
    angle = sign * 2.0 * math.pi * numerator / denominator
    cos, sin = math.cos(angle), math.sin(angle)
    if 8 * numerator % denominator == 0:
        root = math.sqrt(0.5)
        re, im = a
        if cos * sin > 0:
            re, im = re - im, re + im
        else:
            re, im = re + im, im - re
        return (re * (root if cos > 0 else -root), im * (root if cos > 0 else -root))
    return (a[0] * cos - a[1] * sin, a[0] * sin + a[1] * cos)


def fft(points, sign):
    count = len(points)
    if count == 1:
        return points
    if count == 2:
        return [add(points[0], points[1]), sub(points[0], points[1])]
    if count % 4:
        evens, odds = fft(points[0::2], sign), fft(points[1::2], sign)
        turned = [turn_by(odds[k], k, count, sign) for k in range(count // 2)]
        return [add(a, b) for a, b in zip(evens, turned)] + [sub(a, b) for a, b in zip(evens, turned)]
    quarter = count // 4
    parts = [fft(points[r::4], sign) for r in range(4)]
    out = [None] * count
    for k in range(quarter):
        p0, p1, p2, p3 = (turn_by(parts[r][k], r * k, count, sign) for r in range(4))
        s02, d02, s13, d13 = add(p0, p2), sub(p0, p2), add(p1, p3), sub(p1, p3)
        out[k] = add(s02, s13)
        out[k + 2 * quarter] = sub(s02, s13)
        if sign > 0:
            out[k + quarter] = (d02[0] - d13[1], d02[1] + d13[0])
            out[k + 3 * quarter] = (d02[0] + d13[1], d02[1] - d13[0])
        else:
            out[k + quarter] = (d02[0] + d13[1], d02[1] - d13[0])
            out[k + 3 * quarter] = (d02[0] - d13[1], d02[1] + d13[0])
    return out


def outer_forward(load, store, twiddle_ref, outer, half):
    count = outer // 2
    for row in range(0, TILE, HALF_TILE):
        points = []
        for n in range(count):
            near = -2.0 * math.pi * n * (half + 0.25) / outer
            far = -2.0 * math.pi * (n + count) * (half + 0.25) / outer
            a, b = load(n, row), load(n + count, row)
            if n == 0:
                points.append((a + b * math.cos(far), b * math.sin(far)))
            else:
                points.append((a * math.cos(near) + b * math.cos(far), a * math.sin(near) + b * math.sin(far)))
        for k, (re, im) in enumerate(fft(points, -1)):
            at = half * count + k
            cos, sin = twiddle_ref[at, 0:1, :], twiddle_ref[at, 1:2, :]
            store(at, row, re * cos + im * sin, im * cos - re * sin)


def outer_inverse(spec_ref, twiddle_ref, out_ref, outer, half):
    count = outer // 2
    for row in range(0, TILE, HALF_TILE):
        points = []
        for k in range(count):
            at = half * count + k
            rows = pl.ds(at * TILE + row, HALF_TILE)
            re, im = spec_ref[rows, 0:LANES], spec_ref[rows, LANES : 2 * LANES]
            cos, sin = twiddle_ref[at, 0:1, :], twiddle_ref[at, 1:2, :]
            points.append((re * cos - im * sin, re * sin + im * cos))
        for n, (re, im) in enumerate(fft(points, 1)):
            for place in (n, n + count):
                angle = 2.0 * math.pi * place * (half + 0.25) / outer
                value = re if place == 0 else re * math.cos(angle) - im * math.sin(angle)
                if half == 0:
                    out_ref[place, row : row + HALF_TILE, :] = value
                else:
                    out_ref[place, row : row + HALF_TILE, :] += value


def matmul(values, high_ref, low_ref):
    high = values.astype(jnp.bfloat16)
    low = (values - high.astype(jnp.float32)).astype(jnp.bfloat16)
    dot = functools.partial(jnp.dot, preferred_element_type=jnp.float32)
    both = dot(jnp.concatenate([high, low], axis=0), high_ref[...])
    count = high.shape[0]
    return both[:count] + both[count:] + dot(high, low_ref[...])


def order_of(what, parts):
    near = list(range(1, parts))
    return {"grad": near[-1:] + near[:-1], "input": near, "back": near[::-1]}[what]


def places_of(what, parts):
    me = lax.axis_index("ctx")
    return [me ^ k for k in [0, *order_of(what, parts)]]


def put(work_ref, at, row, re, im):
    rows = pl.ds(at * TILE + row, HALF_TILE)
    work_ref[rows, 0:LANES] = re
    work_ref[rows, LANES : 2 * LANES] = im


def spectrum_kernel(taps_ref, *refs, outer, parts, pencil, tables):
    table_refs, refs = refs[:tables], refs[tables:]
    *moved, spec_ref = refs[: -3 - tables]
    tables_here, (taps_here, work_ref, sems) = refs[-3 - tables : -3], refs[-3:]
    high_here, low_here, twiddle_here = tables_here[:3]
    count = outer // 2
    steps = taps_ref.shape[0] // TILE

    def fetch(step):
        rows = pl.ds(step * TILE, TILE)
        return pltpu.make_async_copy(taps_ref.at[rows, :], taps_here.at[rows, :], sems.at[step])

    copies = [
        pltpu.make_async_copy(table_ref, here, sems.at[steps + at])
        for at, (table_ref, here) in enumerate(zip(table_refs, tables_here))
    ]
    copies, later = copies[:3], copies[3:]
    if moved:
        input_ref, grad_ref, *slices, own_grad = moved
        places = places_of("input", parts)
        moves = [(input_ref, *move) for move in zip(places, slices)] + [(grad_ref, places[0], own_grad)]
        for at, (source, place, ref) in enumerate(moves):
            rows = pl.ds(place * pencil, pencil)
            later.append(pltpu.make_async_copy(source.at[rows, :], ref, sems.at[steps + tables + at]))
    fetch(0).start()
    for copy in reversed(copies):
        copy.start()
    for step in range(1, steps):
        fetch(step).start()
    for copy in later:
        copy.start()
    for copy in copies:
        copy.wait()

    @pl.loop(0, steps)
    def _(step):
        fetch(step).wait()

        def load(n, row):
            return taps_here[pl.ds(pl.multiple_of(step * TILE + row, HALF_TILE), HALF_TILE), n * LANES : (n + 1) * LANES]

        for half in range(2):
            outer_forward(load, functools.partial(put, work_ref), twiddle_here, outer, half)
        for half in range(2):
            rows = pl.ds(half * count * TILE, count * TILE)
            spec_ref[step, rows, :] = matmul(work_ref[rows, :], high_here, low_here)

    for copy in later:
        copy.wait()


def correlate(step, piece_refs, places, mate_ref, keep_ref, signal_is_grad, tables, fill_ref, work_ref, out_ref, outer):
    ahead_high, ahead_low, back_high, back_low, twiddle_ref = tables
    count = outer // 2
    per_piece = outer // len(piece_refs)
    rows = pl.ds(pl.multiple_of(step * TILE, TILE), TILE)
    for place, ref in zip(places, piece_refs):
        first = place * per_piece
        for i in range(per_piece):
            fill_ref[first + i] = ref[rows, i * LANES : (i + 1) * LANES].astype(jnp.float32)

    def load(n, row):
        return fill_ref[n, row : row + HALF_TILE, :]

    for half in range(2):
        outer_forward(load, functools.partial(put, work_ref), twiddle_ref, outer, half)
    for half in range(2):
        rows = pl.ds(half * count * TILE, count * TILE)
        own = matmul(work_ref[rows, :], ahead_high, ahead_low)
        if keep_ref is not None:
            keep_ref[step, rows, :] = own
        mate = mate_ref[step, rows, :]
        grad, other = (own, mate) if signal_is_grad else (mate, own)
        grad_re, grad_im = grad[:, :LANES], grad[:, LANES:]
        other_re, other_im = other[:, :LANES], other[:, LANES:]
        both = jnp.concatenate(
            [other_re * grad_re + other_im * grad_im, other_re * grad_im - other_im * grad_re], axis=1
        )
        work_ref[rows, :] = matmul(both, back_high, back_low)
    for half in range(2):
        outer_inverse(work_ref, twiddle_ref, out_ref, outer, half)


def input_kernel(*refs, outer, parts):
    pieces, (mate_ref, *tables) = refs[:parts], refs[parts : parts + 6]
    keep_ref, *sends = refs[parts + 6 : 2 * parts + 7]
    fill_ref, work_ref, out_ref = refs[2 * parts + 7 :]
    places, send_places = places_of("grad", parts), places_of("back", parts)
    per_piece = outer // parts

    @pl.loop(0, pieces[0].shape[0] // TILE)
    def _(step):
        correlate(step, pieces, places, mate_ref, keep_ref, True, tables, fill_ref, work_ref, out_ref, outer)
        rows = pl.ds(pl.multiple_of(step * TILE, TILE), TILE)
        for place, ref in zip(send_places, sends):
            first = place * per_piece
            for i in range(per_piece):
                ref[rows, i * LANES : (i + 1) * LANES] = out_ref[first + i].astype(jnp.bfloat16)


def filter_kernel(*refs, outer, parts):
    pieces, (mate_ref, *tables) = refs[:parts], refs[parts : parts + 6]
    *moved, fill_ref, work_ref, out_ref, result_here, sems = refs[parts + 6 :]
    own_ref, result_ref, whole_ref = moved if len(moved) == 3 else (None, *moved, None)
    places = places_of("input", parts)
    steps = pieces[0].shape[0] // TILE
    if own_ref is not None:
        rows = pl.ds(places[0] * own_ref.shape[0], own_ref.shape[0])
        own_copy = pltpu.make_async_copy(own_ref, whole_ref.at[rows, :], sems.at[steps])
        own_copy.start()

    def flush(step):
        rows = pl.ds(pl.multiple_of(step * TILE, TILE), TILE)
        return pltpu.make_async_copy(result_here.at[rows, :], result_ref.at[rows, :], sems.at[step])

    @pl.loop(0, steps)
    def _(step):
        correlate(step, pieces, places, mate_ref, None, False, tables, fill_ref, work_ref, out_ref, outer)
        rows = pl.ds(pl.multiple_of(step * TILE, TILE), TILE)
        for n in range(outer):
            result_here[rows, n * LANES : (n + 1) * LANES] = out_ref[n]
        flush(step).start()

    @pl.loop(0, steps)
    def _(step):
        flush(step).wait()

    if own_ref is not None:
        own_copy.wait()


def slice_kernel(source_ref, *refs, parts, pencil):
    *blocks, sems = refs
    copies = []
    for place, ref in zip(places_of("grad", parts)[2:], blocks):
        rows = pl.ds(place * pencil, pencil)
        copies.append(pltpu.make_async_copy(source_ref.at[rows, :], ref, sems.at[len(copies)]))
    for copy in copies:
        copy.start()
    for copy in copies:
        copy.wait()


def gather_kernel(held_ref, *refs, pencil):
    *pieces, out_ref, sems = refs
    copies = []
    for place, ref in zip(places_of("back", len(pieces) + 1)[1:], pieces):
        rows = pl.ds(place * pencil, pencil)
        copies.append(pltpu.make_async_copy(ref, out_ref.at[rows, :], sems.at[len(copies)]))
    for copy in copies:
        copy.start()
    for copy in copies:
        copy.wait()


def shards(layer_input, grad_output, filter_taps):
    parts = lax.axis_size("ctx")
    pencil, piece = layer_input.shape[0] // parts, layer_input.shape[1]
    length = piece * parts
    outer = length // LANES
    aligned = pencil % TILE == 0
    rows = -(-pencil // TILE) * TILE
    steps = rows // TILE
    ahead, back, back_scaled, twiddle = dft_tables(length)
    def exchange(what, blocks):
        pairs = [[(i, i ^ k) for i in range(parts)] for k in order_of(what, parts)]
        return [lax.ppermute(block, "ctx", pair) for block, pair in zip(blocks, pairs)]

    def pick(array, place):
        blocks = array.reshape(parts, pencil, piece)
        return lax.dynamic_index_in_dim(blocks, place, 0, keepdims=False)

    def pad(block):
        return block if aligned else jnp.pad(block, ((0, rows - pencil), (0, 0)))

    here = pl.BlockSpec(memory_space=pltpu.VMEM)
    there = pl.BlockSpec(memory_space=pl.ANY)
    spec_shape = jax.ShapeDtypeStruct((steps, outer * TILE, 2 * LANES), jnp.float32)
    slice_shape = jax.ShapeDtypeStruct((rows, piece), jnp.bfloat16)
    work = pltpu.VMEM((outer * TILE, 2 * LANES), jnp.float32)
    lane_tiles = pltpu.VMEM((outer, TILE, LANES), jnp.float32)
    params = pltpu.CompilerParams(vmem_limit_bytes=16 * 1024 * 1024)
    stage_flops = 2 * 3 * rows * outer * (2 * LANES) ** 2
    spec_bytes = 4 * rows * length * 2

    def cost(stages, moved):
        return pl.CostEstimate(flops=stages * stage_flops, bytes_accessed=moved, transcendentals=0)

    def in_hbm(array):
        return pltpu.with_memory_space_constraint(array, pltpu.HBM)

    own, *others = places_of("grad", parts)
    if aligned:
        blocks = pl.pallas_call(
            functools.partial(slice_kernel, parts=parts, pencil=pencil),
            in_specs=[there],
            out_specs=[here] * (parts - 2),
            out_shape=[slice_shape] * (parts - 2),
            scratch_shapes=[pltpu.SemaphoreType.DMA((parts - 2,))],
            cost_estimate=cost(0, 2 * (parts - 2) * pencil * piece * 2),
            name="slice_grad",
        )(in_hbm(grad_output))
    else:
        blocks = [pick(grad_output, place) for place in others[1:]]
    grad_pieces = exchange("grad", [pick(grad_output, others[0]), *blocks])

    taps = filter_taps.reshape(pencil, length)
    tables = [*ahead, twiddle, *back, *back_scaled]
    slices = parts + 1 if aligned else 0
    results = pl.pallas_call(
        functools.partial(spectrum_kernel, outer=outer, parts=parts, pencil=pencil, tables=len(tables)),
        in_specs=[there] * (1 + len(tables) + (2 if aligned else 0)),
        out_specs=[here] * (slices + 1 + len(tables)),
        out_shape=[slice_shape] * slices + [spec_shape] + [jax.ShapeDtypeStruct(table.shape, table.dtype) for table in tables],
        scratch_shapes=[
            pltpu.VMEM((rows, length), jnp.float32),
            work,
            pltpu.SemaphoreType.DMA((steps + len(tables) + slices,)),
        ],
        compiler_params=params,
        cost_estimate=cost(1, 2 * spec_bytes),
        name="taps_spectrum",
    )(*map(in_hbm, [pad(taps), *map(jnp.asarray, tables), *([layer_input, grad_output] if aligned else [])]))
    taps_spectrum, *tables = results[slices:]
    ahead, twiddle, back, back_scaled = tables[:2], tables[2], tables[3:5], tables[5:]
    blocks = results[:parts] if aligned else [pick(layer_input, place) for place in places_of("input", parts)]
    grad_pieces = [results[parts] if aligned else pick(grad_output, own), *grad_pieces]
    input_pieces = [blocks[0], *exchange("input", blocks[1:])]

    tables = [*ahead, *back, twiddle]
    grad_spectrum, *outgoing = pl.pallas_call(
        functools.partial(input_kernel, outer=outer, parts=parts),
        in_specs=[here] * (parts + 1 + len(tables)),
        out_specs=[here] * (parts + 1),
        out_shape=[spec_shape, *[slice_shape] * parts],
        scratch_shapes=[lane_tiles, work, lane_tiles],
        compiler_params=params,
        cost_estimate=cost(2, 2 * spec_bytes),
        name="grad_input",
    )(*map(pad, grad_pieces), taps_spectrum, *tables)

    outgoing = [block[:pencil] for block in outgoing]
    incoming = [outgoing[0], *exchange("back", outgoing[1:])]

    tables = [*ahead, *back_scaled, twiddle]
    filter_shape = jax.ShapeDtypeStruct((rows, length), jnp.float32)
    whole_shape = jax.ShapeDtypeStruct((parts * pencil, piece), jnp.bfloat16)
    grad_filter, *whole = pl.pallas_call(
        functools.partial(filter_kernel, outer=outer, parts=parts),
        in_specs=[here] * (parts + 1 + len(tables) + aligned),
        out_specs=[there] * (1 + aligned),
        out_shape=[filter_shape, whole_shape][: 1 + aligned],
        scratch_shapes=[
            lane_tiles,
            work,
            lane_tiles,
            pltpu.VMEM((rows, length), jnp.float32),
            pltpu.SemaphoreType.DMA((steps + aligned,)),
        ],
        compiler_params=params,
        cost_estimate=cost(2, 2 * spec_bytes),
        name="grad_filter",
    )(*map(pad, input_pieces), grad_spectrum, *tables, *incoming[:aligned])

    if aligned:
        grad_input = pl.pallas_call(
            functools.partial(gather_kernel, pencil=pencil),
            in_specs=[there] * parts,
            out_specs=there,
            out_shape=whole_shape,
            input_output_aliases={0: 0},
            scratch_shapes=[pltpu.SemaphoreType.DMA((parts - 1,))],
            name="gather_pieces",
        )(*whole, *[pltpu.with_memory_space_constraint(block, pltpu.VMEM) for block in incoming[1:]])
    else:
        grad_input = jnp.zeros((parts, pencil, piece), jnp.bfloat16)
        for place, block in zip(places_of("back", parts), incoming):
            grad_input = lax.dynamic_update_index_in_dim(grad_input, block, place, 0)
        grad_input = grad_input.reshape(parts * pencil, piece)
    return (grad_input, grad_filter[:pencil].reshape(1, pencil, length))


def solution(mesh):
    in_specs = (P(("dp", "chan"), "ctx"), P(("dp", "chan"), "ctx"), P(("dp", "chan"), "ctx", None))
    out_specs = (P(("dp", "chan"), "ctx"), P(("dp", "chan"), "ctx", None))
    return jax.shard_map(shards, mesh=mesh, in_specs=in_specs, out_specs=out_specs, check_vma=False)
```

```python
import functools
import math

import jax
import jax.numpy as jnp
import ml_dtypes
import numpy as np
from jax import lax
from jax.experimental import pallas as pl
from jax.experimental.pallas import tpu as pltpu
from jax.sharding import PartitionSpec as P

LANES = 128
TILE = 16
HALF_TILE = 8


def split_table(table):
    high = table.astype(ml_dtypes.bfloat16)
    low = (table - high.astype(np.float64)).astype(ml_dtypes.bfloat16)
    return high, low


def dft_tables(length):
    index = np.arange(LANES)
    angle = 2.0 * np.pi * (np.outer(index, index) % LANES) / LANES
    cos, sin = np.cos(angle), np.sin(angle)
    ahead = np.block([[cos, -sin], [sin, cos]])
    back = np.block([[cos, sin], [-sin, cos]]) / length
    outer = length // LANES
    order = np.concatenate([np.arange(0, outer, 2), np.arange(1, outer, 2)])
    turn = 2.0 * np.pi * np.outer(order + 0.25, index) / length
    twiddle = np.stack([np.cos(turn), np.sin(turn)], axis=1).astype(np.float32)
    return split_table(ahead), split_table(back), split_table(back / math.sqrt(length)), twiddle


def add(a, b):
    return (a[0] + b[0], a[1] + b[1])


def sub(a, b):
    return (a[0] - b[0], a[1] - b[1])


def turn_quarter(a, sign):
    return (-a[1], a[0]) if sign > 0 else (a[1], -a[0])


def turn_by(a, numerator, denominator, sign):
    numerator = numerator % denominator
    if numerator == 0:
        return a
    if 4 * numerator == denominator:
        return turn_quarter(a, sign)
    if 2 * numerator == denominator:
        return (-a[0], -a[1])
    if 4 * numerator == 3 * denominator:
        return turn_quarter(a, -sign)
    angle = sign * 2.0 * math.pi * numerator / denominator
    cos, sin = math.cos(angle), math.sin(angle)
    if 8 * numerator % denominator == 0:
        root = math.sqrt(0.5)
        re, im = a
        if cos * sin > 0:
            re, im = re - im, re + im
        else:
            re, im = re + im, im - re
        return (re * (root if cos > 0 else -root), im * (root if cos > 0 else -root))
    return (a[0] * cos - a[1] * sin, a[0] * sin + a[1] * cos)


def fft(points, sign):
    count = len(points)
    if count == 1:
        return points
    if count == 2:
        return [add(points[0], points[1]), sub(points[0], points[1])]
    if count % 4:
        evens, odds = fft(points[0::2], sign), fft(points[1::2], sign)
        turned = [turn_by(odds[k], k, count, sign) for k in range(count // 2)]
        return [add(a, b) for a, b in zip(evens, turned)] + [sub(a, b) for a, b in zip(evens, turned)]
    quarter = count // 4
    parts = [fft(points[r::4], sign) for r in range(4)]
    out = [None] * count
    for k in range(quarter):
        p0, p1, p2, p3 = (turn_by(parts[r][k], r * k, count, sign) for r in range(4))
        s02, d02, s13, d13 = add(p0, p2), sub(p0, p2), add(p1, p3), sub(p1, p3)
        out[k] = add(s02, s13)
        out[k + 2 * quarter] = sub(s02, s13)
        if sign > 0:
            out[k + quarter] = (d02[0] - d13[1], d02[1] + d13[0])
            out[k + 3 * quarter] = (d02[0] + d13[1], d02[1] - d13[0])
        else:
            out[k + quarter] = (d02[0] + d13[1], d02[1] - d13[0])
            out[k + 3 * quarter] = (d02[0] - d13[1], d02[1] + d13[0])
    return out


def outer_forward(load, store, twiddle_ref, outer, half):
    count = outer // 2
    for row in range(0, TILE, HALF_TILE):
        points = []
        for n in range(count):
            near = -2.0 * math.pi * n * (half + 0.25) / outer
            far = -2.0 * math.pi * (n + count) * (half + 0.25) / outer
            a, b = load(n, row), load(n + count, row)
            if n == 0:
                points.append((a + b * math.cos(far), b * math.sin(far)))
            else:
                points.append((a * math.cos(near) + b * math.cos(far), a * math.sin(near) + b * math.sin(far)))
        for k, (re, im) in enumerate(fft(points, -1)):
            at = half * count + k
            cos, sin = twiddle_ref[at, 0:1, :], twiddle_ref[at, 1:2, :]
            store(at, row, re * cos + im * sin, im * cos - re * sin)


def outer_inverse(spec_ref, twiddle_ref, out_ref, outer, half):
    count = outer // 2
    for row in range(0, TILE, HALF_TILE):
        points = []
        for k in range(count):
            at = half * count + k
            rows = pl.ds(at * TILE + row, HALF_TILE)
            re, im = spec_ref[rows, 0:LANES], spec_ref[rows, LANES : 2 * LANES]
            cos, sin = twiddle_ref[at, 0:1, :], twiddle_ref[at, 1:2, :]
            points.append((re * cos - im * sin, re * sin + im * cos))
        for n, (re, im) in enumerate(fft(points, 1)):
            for place in (n, n + count):
                angle = 2.0 * math.pi * place * (half + 0.25) / outer
                value = re if place == 0 else re * math.cos(angle) - im * math.sin(angle)
                if half == 0:
                    out_ref[place, row : row + HALF_TILE, :] = value
                else:
                    out_ref[place, row : row + HALF_TILE, :] += value


def matmul(values, high_ref, low_ref):
    high = values.astype(jnp.bfloat16)
    low = (values - high.astype(jnp.float32)).astype(jnp.bfloat16)
    dot = functools.partial(jnp.dot, preferred_element_type=jnp.float32)
    both = dot(jnp.concatenate([high, low], axis=0), high_ref[...])
    count = high.shape[0]
    return both[:count] + both[count:] + dot(high, low_ref[...])


def order_of(what, parts):
    near = list(range(1, parts))
    return {"grad": near[-1:] + near[:-1], "input": near, "back": near[::-1]}[what]


def places_of(what, parts):
    me = lax.axis_index("ctx")
    return [me ^ k for k in [0, *order_of(what, parts)]]


def put(work_ref, at, row, re, im):
    rows = pl.ds(at * TILE + row, HALF_TILE)
    work_ref[rows, 0:LANES] = re
    work_ref[rows, LANES : 2 * LANES] = im


def spectrum_kernel(taps_ref, *refs, outer, tables):
    table_refs, spec_ref, tables_here = refs[:tables], refs[tables], refs[tables + 1 : -3]
    taps_here, work_ref, sems = refs[-3:]
    high_here, low_here, twiddle_here = tables_here[:3]
    count = outer // 2
    steps = taps_ref.shape[0] // TILE

    def fetch(step):
        rows = pl.ds(step * TILE, TILE)
        return pltpu.make_async_copy(taps_ref.at[rows, :], taps_here.at[rows, :], sems.at[step])

    copies = [
        pltpu.make_async_copy(table_ref, here, sems.at[steps + at])
        for at, (table_ref, here) in enumerate(zip(table_refs, tables_here))
    ]
    copies, later = copies[:3], copies[3:]
    fetch(0).start()
    for copy in reversed(copies):
        copy.start()
    for step in range(1, steps):
        fetch(step).start()
    for copy in later:
        copy.start()
    for copy in copies:
        copy.wait()

    @pl.loop(0, steps)
    def _(step):
        fetch(step).wait()

        def load(n, row):
            return taps_here[pl.ds(pl.multiple_of(step * TILE + row, HALF_TILE), HALF_TILE), n * LANES : (n + 1) * LANES]

        for half in range(2):
            outer_forward(load, functools.partial(put, work_ref), twiddle_here, outer, half)
        for half in range(2):
            rows = pl.ds(half * count * TILE, count * TILE)
            spec_ref[step, rows, :] = matmul(work_ref[rows, :], high_here, low_here)

    for copy in later:
        copy.wait()


def correlate(step, piece_refs, places, mate_ref, keep_ref, signal_is_grad, tables, fill_ref, work_ref, out_ref, outer):
    ahead_high, ahead_low, back_high, back_low, twiddle_ref = tables
    count = outer // 2
    per_piece = outer // len(piece_refs)
    rows = pl.ds(pl.multiple_of(step * TILE, TILE), TILE)
    for place, ref in zip(places, piece_refs):
        first = place * per_piece
        for i in range(per_piece):
            fill_ref[first + i] = ref[rows, i * LANES : (i + 1) * LANES].astype(jnp.float32)

    def load(n, row):
        return fill_ref[n, row : row + HALF_TILE, :]

    for half in range(2):
        outer_forward(load, functools.partial(put, work_ref), twiddle_ref, outer, half)
    for half in range(2):
        rows = pl.ds(half * count * TILE, count * TILE)
        own = matmul(work_ref[rows, :], ahead_high, ahead_low)
        if keep_ref is not None:
            keep_ref[step, rows, :] = own
        mate = mate_ref[step, rows, :]
        grad, other = (own, mate) if signal_is_grad else (mate, own)
        grad_re, grad_im = grad[:, :LANES], grad[:, LANES:]
        other_re, other_im = other[:, :LANES], other[:, LANES:]
        both = jnp.concatenate(
            [other_re * grad_re + other_im * grad_im, other_re * grad_im - other_im * grad_re], axis=1
        )
        work_ref[rows, :] = matmul(both, back_high, back_low)
    for half in range(2):
        outer_inverse(work_ref, twiddle_ref, out_ref, outer, half)


def input_kernel(*refs, outer, parts):
    pieces, (mate_ref, *tables) = refs[:parts], refs[parts : parts + 6]
    keep_ref, *sends = refs[parts + 6 : 2 * parts + 7]
    fill_ref, work_ref, out_ref = refs[2 * parts + 7 :]
    places, send_places = places_of("grad", parts), places_of("back", parts)
    per_piece = outer // parts

    @pl.loop(0, pieces[0].shape[0] // TILE)
    def _(step):
        correlate(step, pieces, places, mate_ref, keep_ref, True, tables, fill_ref, work_ref, out_ref, outer)
        rows = pl.ds(pl.multiple_of(step * TILE, TILE), TILE)
        for place, ref in zip(send_places, sends):
            first = place * per_piece
            for i in range(per_piece):
                ref[rows, i * LANES : (i + 1) * LANES] = out_ref[first + i].astype(jnp.bfloat16)


def filter_kernel(*refs, outer, parts):
    pieces, (mate_ref, *tables) = refs[:parts], refs[parts : parts + 6]
    *moved, fill_ref, work_ref, out_ref, result_here, sems = refs[parts + 6 :]
    own_ref, result_ref, whole_ref = moved if len(moved) == 3 else (None, *moved, None)
    places = places_of("input", parts)
    steps = pieces[0].shape[0] // TILE
    if own_ref is not None:
        rows = pl.ds(places[0] * own_ref.shape[0], own_ref.shape[0])
        own_copy = pltpu.make_async_copy(own_ref, whole_ref.at[rows, :], sems.at[steps])
        own_copy.start()

    def flush(step):
        rows = pl.ds(pl.multiple_of(step * TILE, TILE), TILE)
        return pltpu.make_async_copy(result_here.at[rows, :], result_ref.at[rows, :], sems.at[step])

    @pl.loop(0, steps)
    def _(step):
        correlate(step, pieces, places, mate_ref, None, False, tables, fill_ref, work_ref, out_ref, outer)
        rows = pl.ds(pl.multiple_of(step * TILE, TILE), TILE)
        for n in range(outer):
            result_here[rows, n * LANES : (n + 1) * LANES] = out_ref[n]
        flush(step).start()

    @pl.loop(0, steps)
    def _(step):
        flush(step).wait()

    if own_ref is not None:
        own_copy.wait()


def slice_kernel(grad_ref, input_ref, *refs, parts, pencil):
    *blocks, sems = refs
    grad_places, input_places = places_of("grad", parts), places_of("input", parts)
    moves = [(grad_ref, place) for place in grad_places[2:] + grad_places[:1]]
    moves += [(input_ref, place) for place in input_places]
    copies = []
    for (source_ref, place), ref in zip(moves, blocks):
        rows = pl.ds(place * pencil, pencil)
        copies.append(pltpu.make_async_copy(source_ref.at[rows, :], ref, sems.at[len(copies)]))
    for copy in copies:
        copy.start()
    for copy in copies:
        copy.wait()


def gather_kernel(held_ref, *refs, first, parts, pencil):
    *pieces, out_ref, sems = refs
    copies = []
    for place, ref in zip(places_of("back", parts)[first:], pieces):
        rows = pl.ds(place * pencil, pencil)
        copies.append(pltpu.make_async_copy(ref, out_ref.at[rows, :], sems.at[len(copies)]))
    for copy in copies:
        copy.start()
    for copy in copies:
        copy.wait()


def shards(layer_input, grad_output, filter_taps):
    parts = lax.axis_size("ctx")
    pencil, piece = layer_input.shape[0] // parts, layer_input.shape[1]
    length = piece * parts
    outer = length // LANES
    aligned = pencil % TILE == 0
    rows = -(-pencil // TILE) * TILE
    steps = rows // TILE
    ahead, back, back_scaled, twiddle = dft_tables(length)
    def exchange(what, blocks):
        pairs = [[(i, i ^ k) for i in range(parts)] for k in order_of(what, parts)]
        return [lax.ppermute(block, "ctx", pair) for block, pair in zip(blocks, pairs)]

    def pick(array, place):
        blocks = array.reshape(parts, pencil, piece)
        return lax.dynamic_index_in_dim(blocks, place, 0, keepdims=False)

    def pad(block):
        return block if aligned else jnp.pad(block, ((0, rows - pencil), (0, 0)))

    here = pl.BlockSpec(memory_space=pltpu.VMEM)
    there = pl.BlockSpec(memory_space=pl.ANY)
    spec_shape = jax.ShapeDtypeStruct((steps, outer * TILE, 2 * LANES), jnp.float32)
    slice_shape = jax.ShapeDtypeStruct((rows, piece), jnp.bfloat16)
    work = pltpu.VMEM((outer * TILE, 2 * LANES), jnp.float32)
    lane_tiles = pltpu.VMEM((outer, TILE, LANES), jnp.float32)
    params = pltpu.CompilerParams(vmem_limit_bytes=16 * 1024 * 1024)
    stage_flops = 2 * 3 * rows * outer * (2 * LANES) ** 2
    spec_bytes = 4 * rows * length * 2

    def cost(stages, moved):
        return pl.CostEstimate(flops=stages * stage_flops, bytes_accessed=moved, transcendentals=0)

    def in_hbm(array):
        return pltpu.with_memory_space_constraint(array, pltpu.HBM)

    own, *others = places_of("grad", parts)
    if aligned:
        count = 2 * parts - 1
        blocks = pl.pallas_call(
            functools.partial(slice_kernel, parts=parts, pencil=pencil),
            in_specs=[there] * 2,
            out_specs=[here] * count,
            out_shape=[slice_shape] * count,
            scratch_shapes=[pltpu.SemaphoreType.DMA((count,))],
            cost_estimate=cost(0, 2 * count * pencil * piece * 2),
            name="slice_blocks",
        )(in_hbm(grad_output), in_hbm(layer_input))
    else:
        blocks = [pick(grad_output, place) for place in [*others[1:], own]]
        blocks += [pick(layer_input, place) for place in places_of("input", parts)]
    grad_blocks, input_blocks = blocks[: parts - 1], blocks[parts - 1 :]
    grad_pieces = [grad_blocks[-1], *exchange("grad", [pick(grad_output, others[0]), *grad_blocks[:-1]])]
    input_pieces = [input_blocks[0], *exchange("input", input_blocks[1:])]

    taps = filter_taps.reshape(pencil, length)
    tables = [*ahead, twiddle, *back, *back_scaled]
    results = pl.pallas_call(
        functools.partial(spectrum_kernel, outer=outer, tables=len(tables)),
        in_specs=[there] * (1 + len(tables)),
        out_specs=[here] * (1 + len(tables)),
        out_shape=[spec_shape] + [jax.ShapeDtypeStruct(table.shape, table.dtype) for table in tables],
        scratch_shapes=[
            pltpu.VMEM((rows, length), jnp.float32),
            work,
            pltpu.SemaphoreType.DMA((steps + len(tables),)),
        ],
        compiler_params=params,
        cost_estimate=cost(1, 2 * spec_bytes),
        name="taps_spectrum",
    )(*map(in_hbm, [pad(taps), *map(jnp.asarray, tables)]))
    taps_spectrum, *tables = results
    ahead, twiddle, back, back_scaled = tables[:2], tables[2], tables[3:5], tables[5:]
    tables = [*ahead, *back, twiddle]
    grad_spectrum, *outgoing = pl.pallas_call(
        functools.partial(input_kernel, outer=outer, parts=parts),
        in_specs=[here] * (parts + 1 + len(tables)),
        out_specs=[here] * (parts + 1),
        out_shape=[spec_shape, *[slice_shape] * parts],
        scratch_shapes=[lane_tiles, work, lane_tiles],
        compiler_params=params,
        cost_estimate=cost(2, 2 * spec_bytes),
        name="grad_input",
    )(*map(pad, grad_pieces), taps_spectrum, *tables)

    outgoing = [block[:pencil] for block in outgoing]
    incoming = [outgoing[0], *exchange("back", outgoing[1:])]

    tables = [*ahead, *back_scaled, twiddle]
    filter_shape = jax.ShapeDtypeStruct((rows, length), jnp.float32)
    whole_shape = jax.ShapeDtypeStruct((parts * pencil, piece), jnp.bfloat16)
    grad_filter, *whole = pl.pallas_call(
        functools.partial(filter_kernel, outer=outer, parts=parts),
        in_specs=[here] * (parts + 1 + len(tables) + aligned),
        out_specs=[there] * (1 + aligned),
        out_shape=[filter_shape, whole_shape][: 1 + aligned],
        scratch_shapes=[
            lane_tiles,
            work,
            lane_tiles,
            pltpu.VMEM((rows, length), jnp.float32),
            pltpu.SemaphoreType.DMA((steps + aligned,)),
        ],
        compiler_params=params,
        cost_estimate=cost(2, 2 * spec_bytes),
        name="grad_filter",
    )(*map(pad, input_pieces), grad_spectrum, *tables, *incoming[:aligned])

    if aligned:
        (grad_input,) = whole
        for first, last in ((1, 2), (2, parts)):
            blocks = [pltpu.with_memory_space_constraint(block, pltpu.VMEM) for block in incoming[first:last]]
            grad_input = pl.pallas_call(
                functools.partial(gather_kernel, first=first, parts=parts, pencil=pencil),
                in_specs=[there] * (1 + len(blocks)),
                out_specs=there,
                out_shape=whole_shape,
                input_output_aliases={0: 0},
                scratch_shapes=[pltpu.SemaphoreType.DMA((len(blocks),))],
                name="gather_pieces",
            )(grad_input, *blocks)
    else:
        grad_input = jnp.zeros((parts, pencil, piece), jnp.bfloat16)
        for place, block in zip(places_of("back", parts), incoming):
            grad_input = lax.dynamic_update_index_in_dim(grad_input, block, place, 0)
        grad_input = grad_input.reshape(parts * pencil, piece)
    return (grad_input, grad_filter[:pencil].reshape(1, pencil, length))


def solution(mesh):
    in_specs = (P(("dp", "chan"), "ctx"), P(("dp", "chan"), "ctx"), P(("dp", "chan"), "ctx", None))
    out_specs = (P(("dp", "chan"), "ctx"), P(("dp", "chan"), "ctx", None))
    return jax.shard_map(shards, mesh=mesh, in_specs=in_specs, out_specs=out_specs, check_vma=False)
```

```python
import functools
import math

import jax
import jax.numpy as jnp
import ml_dtypes
import numpy as np
from jax import lax
from jax.experimental import pallas as pl
from jax.experimental.pallas import tpu as pltpu
from jax.sharding import PartitionSpec as P

LANES = 128
TILE = 16
HALF_TILE = 8


def split_table(table):
    high = table.astype(ml_dtypes.bfloat16)
    low = (table - high.astype(np.float64)).astype(ml_dtypes.bfloat16)
    return high, low


def dft_tables(length):
    index = np.arange(LANES)
    angle = 2.0 * np.pi * (np.outer(index, index) % LANES) / LANES
    cos, sin = np.cos(angle), np.sin(angle)
    ahead = np.block([[cos, -sin], [sin, cos]])
    back = np.block([[cos, sin], [-sin, cos]]) / length
    outer = length // LANES
    order = np.concatenate([np.arange(0, outer, 2), np.arange(1, outer, 2)])
    turn = 2.0 * np.pi * np.outer(order + 0.25, index) / length
    twiddle = np.stack([np.cos(turn), np.sin(turn)], axis=1).astype(np.float32)
    return split_table(ahead), split_table(back), split_table(back / math.sqrt(length)), twiddle


def add(a, b):
    return (a[0] + b[0], a[1] + b[1])


def sub(a, b):
    return (a[0] - b[0], a[1] - b[1])


def turn_quarter(a, sign):
    return (-a[1], a[0]) if sign > 0 else (a[1], -a[0])


def turn_by(a, numerator, denominator, sign):
    numerator = numerator % denominator
    if numerator == 0:
        return a
    if 4 * numerator == denominator:
        return turn_quarter(a, sign)
    if 2 * numerator == denominator:
        return (-a[0], -a[1])
    if 4 * numerator == 3 * denominator:
        return turn_quarter(a, -sign)
    angle = sign * 2.0 * math.pi * numerator / denominator
    cos, sin = math.cos(angle), math.sin(angle)
    if 8 * numerator % denominator == 0:
        root = math.sqrt(0.5)
        re, im = a
        if cos * sin > 0:
            re, im = re - im, re + im
        else:
            re, im = re + im, im - re
        return (re * (root if cos > 0 else -root), im * (root if cos > 0 else -root))
    return (a[0] * cos - a[1] * sin, a[0] * sin + a[1] * cos)


def fft(points, sign):
    count = len(points)
    if count == 1:
        return points
    if count == 2:
        return [add(points[0], points[1]), sub(points[0], points[1])]
    if count % 4:
        evens, odds = fft(points[0::2], sign), fft(points[1::2], sign)
        turned = [turn_by(odds[k], k, count, sign) for k in range(count // 2)]
        return [add(a, b) for a, b in zip(evens, turned)] + [sub(a, b) for a, b in zip(evens, turned)]
    quarter = count // 4
    parts = [fft(points[r::4], sign) for r in range(4)]
    out = [None] * count
    for k in range(quarter):
        p0, p1, p2, p3 = (turn_by(parts[r][k], r * k, count, sign) for r in range(4))
        s02, d02, s13, d13 = add(p0, p2), sub(p0, p2), add(p1, p3), sub(p1, p3)
        out[k] = add(s02, s13)
        out[k + 2 * quarter] = sub(s02, s13)
        if sign > 0:
            out[k + quarter] = (d02[0] - d13[1], d02[1] + d13[0])
            out[k + 3 * quarter] = (d02[0] + d13[1], d02[1] - d13[0])
        else:
            out[k + quarter] = (d02[0] + d13[1], d02[1] - d13[0])
            out[k + 3 * quarter] = (d02[0] - d13[1], d02[1] + d13[0])
    return out


def outer_forward(load, store, twiddle_ref, outer, half):
    count = outer // 2
    for row in range(0, TILE, HALF_TILE):
        points = []
        for n in range(count):
            near = -2.0 * math.pi * n * (half + 0.25) / outer
            far = -2.0 * math.pi * (n + count) * (half + 0.25) / outer
            a, b = load(n, row), load(n + count, row)
            if n == 0:
                points.append((a + b * math.cos(far), b * math.sin(far)))
            else:
                points.append((a * math.cos(near) + b * math.cos(far), a * math.sin(near) + b * math.sin(far)))
        for k, (re, im) in enumerate(fft(points, -1)):
            at = half * count + k
            cos, sin = twiddle_ref[at, 0:1, :], twiddle_ref[at, 1:2, :]
            store(at, row, re * cos + im * sin, im * cos - re * sin)


def outer_inverse(spec_ref, twiddle_ref, out_ref, outer, half):
    count = outer // 2
    for row in range(0, TILE, HALF_TILE):
        points = []
        for k in range(count):
            at = half * count + k
            rows = pl.ds(at * TILE + row, HALF_TILE)
            re, im = spec_ref[rows, 0:LANES], spec_ref[rows, LANES : 2 * LANES]
            cos, sin = twiddle_ref[at, 0:1, :], twiddle_ref[at, 1:2, :]
            points.append((re * cos - im * sin, re * sin + im * cos))
        for n, (re, im) in enumerate(fft(points, 1)):
            for place in (n, n + count):
                angle = 2.0 * math.pi * place * (half + 0.25) / outer
                value = re if place == 0 else re * math.cos(angle) - im * math.sin(angle)
                if half == 0:
                    out_ref[place, row : row + HALF_TILE, :] = value
                else:
                    out_ref[place, row : row + HALF_TILE, :] += value


def matmul(values, high_ref, low_ref):
    high = values.astype(jnp.bfloat16)
    low = (values - high.astype(jnp.float32)).astype(jnp.bfloat16)
    dot = functools.partial(jnp.dot, preferred_element_type=jnp.float32)
    both = dot(jnp.concatenate([high, low], axis=0), high_ref[...])
    count = high.shape[0]
    return both[:count] + both[count:] + dot(high, low_ref[...])


def order_of(what, parts):
    near = list(range(1, parts))
    middle = near[:-1][::-1] + near[-1:]
    return {"grad": near[-1:] + near[:-1], "input": middle, "back": near[::-1]}[what]


def places_of(what, parts):
    me = lax.axis_index("ctx")
    return [me ^ k for k in [0, *order_of(what, parts)]]


def put(work_ref, at, row, re, im):
    rows = pl.ds(at * TILE + row, HALF_TILE)
    work_ref[rows, 0:LANES] = re
    work_ref[rows, LANES : 2 * LANES] = im


def spectrum_kernel(taps_ref, *refs, outer, tables):
    table_refs, spec_ref, tables_here = refs[:tables], refs[tables], refs[tables + 1 : -3]
    taps_here, work_ref, sems = refs[-3:]
    high_here, low_here, twiddle_here = tables_here[:3]
    count = outer // 2
    steps = taps_ref.shape[0] // TILE

    def fetch(step):
        rows = pl.ds(step * TILE, TILE)
        return pltpu.make_async_copy(taps_ref.at[rows, :], taps_here.at[rows, :], sems.at[step])

    copies = [
        pltpu.make_async_copy(table_ref, here, sems.at[steps + at])
        for at, (table_ref, here) in enumerate(zip(table_refs, tables_here))
    ]
    copies, later = copies[:3], copies[3:]
    fetch(0).start()
    for copy in reversed(copies):
        copy.start()
    for step in range(1, steps):
        fetch(step).start()
    for copy in later:
        copy.start()
    for copy in copies:
        copy.wait()

    @pl.loop(0, steps)
    def _(step):
        fetch(step).wait()

        def load(n, row):
            return taps_here[pl.ds(pl.multiple_of(step * TILE + row, HALF_TILE), HALF_TILE), n * LANES : (n + 1) * LANES]

        for half in range(2):
            outer_forward(load, functools.partial(put, work_ref), twiddle_here, outer, half)
        for half in range(2):
            rows = pl.ds(half * count * TILE, count * TILE)
            spec_ref[step, rows, :] = matmul(work_ref[rows, :], high_here, low_here)

    for copy in later:
        copy.wait()


def correlate(step, piece_refs, places, mate_ref, keep_ref, signal_is_grad, tables, fill_ref, work_ref, out_ref, outer):
    ahead_high, ahead_low, back_high, back_low, twiddle_ref = tables
    count = outer // 2
    per_piece = outer // len(piece_refs)
    rows = pl.ds(pl.multiple_of(step * TILE, TILE), TILE)
    for place, ref in zip(places, piece_refs):
        first = place * per_piece
        for i in range(per_piece):
            fill_ref[first + i] = ref[rows, i * LANES : (i + 1) * LANES].astype(jnp.float32)

    def load(n, row):
        return fill_ref[n, row : row + HALF_TILE, :]

    for half in range(2):
        outer_forward(load, functools.partial(put, work_ref), twiddle_ref, outer, half)
    for half in range(2):
        rows = pl.ds(half * count * TILE, count * TILE)
        own = matmul(work_ref[rows, :], ahead_high, ahead_low)
        if keep_ref is not None:
            keep_ref[step, rows, :] = own
        mate = mate_ref[step, rows, :]
        grad, other = (own, mate) if signal_is_grad else (mate, own)
        grad_re, grad_im = grad[:, :LANES], grad[:, LANES:]
        other_re, other_im = other[:, :LANES], other[:, LANES:]
        both = jnp.concatenate(
            [other_re * grad_re + other_im * grad_im, other_re * grad_im - other_im * grad_re], axis=1
        )
        work_ref[rows, :] = matmul(both, back_high, back_low)
    for half in range(2):
        outer_inverse(work_ref, twiddle_ref, out_ref, outer, half)


def input_kernel(*refs, outer, parts):
    pieces, (mate_ref, *tables) = refs[:parts], refs[parts : parts + 6]
    keep_ref, *sends = refs[parts + 6 : 2 * parts + 7]
    fill_ref, work_ref, out_ref = refs[2 * parts + 7 :]
    places, send_places = places_of("grad", parts), places_of("back", parts)
    per_piece = outer // parts

    @pl.loop(0, pieces[0].shape[0] // TILE)
    def _(step):
        correlate(step, pieces, places, mate_ref, keep_ref, True, tables, fill_ref, work_ref, out_ref, outer)
        rows = pl.ds(pl.multiple_of(step * TILE, TILE), TILE)
        for place, ref in zip(send_places, sends):
            first = place * per_piece
            for i in range(per_piece):
                ref[rows, i * LANES : (i + 1) * LANES] = out_ref[first + i].astype(jnp.bfloat16)


def filter_kernel(*refs, outer, parts):
    pieces, (mate_ref, *tables) = refs[:parts], refs[parts : parts + 6]
    *moved, fill_ref, work_ref, out_ref, result_here, sems = refs[parts + 6 :]
    own_ref, result_ref, whole_ref = moved if len(moved) == 3 else (None, *moved, None)
    places = places_of("input", parts)
    steps = pieces[0].shape[0] // TILE
    if own_ref is not None:
        rows = pl.ds(places[0] * own_ref.shape[0], own_ref.shape[0])
        own_copy = pltpu.make_async_copy(own_ref, whole_ref.at[rows, :], sems.at[steps])
        own_copy.start()

    def flush(step):
        rows = pl.ds(pl.multiple_of(step * TILE, TILE), TILE)
        return pltpu.make_async_copy(result_here.at[rows, :], result_ref.at[rows, :], sems.at[step])

    @pl.loop(0, steps)
    def _(step):
        correlate(step, pieces, places, mate_ref, None, False, tables, fill_ref, work_ref, out_ref, outer)
        rows = pl.ds(pl.multiple_of(step * TILE, TILE), TILE)
        for n in range(outer):
            result_here[rows, n * LANES : (n + 1) * LANES] = out_ref[n]
        flush(step).start()

    @pl.loop(0, steps)
    def _(step):
        flush(step).wait()

    if own_ref is not None:
        own_copy.wait()


def slice_kernel(grad_ref, input_ref, *refs, parts, pencil):
    *blocks, sems = refs
    grad_places, input_places = places_of("grad", parts), places_of("input", parts)
    moves = [(grad_ref, place) for place in grad_places[2:] + grad_places[:1]]
    moves += [(input_ref, place) for place in input_places]
    copies = []
    for (source_ref, place), ref in zip(moves, blocks):
        rows = pl.ds(place * pencil, pencil)
        copies.append(pltpu.make_async_copy(source_ref.at[rows, :], ref, sems.at[len(copies)]))
    for copy in copies:
        copy.start()
    for copy in copies:
        copy.wait()


def gather_kernel(held_ref, *refs, first, parts, pencil):
    *pieces, out_ref, sems = refs
    copies = []
    for place, ref in zip(places_of("back", parts)[first:], pieces):
        rows = pl.ds(place * pencil, pencil)
        copies.append(pltpu.make_async_copy(ref, out_ref.at[rows, :], sems.at[len(copies)]))
    for copy in copies:
        copy.start()
    for copy in copies:
        copy.wait()


def shards(layer_input, grad_output, filter_taps):
    parts = lax.axis_size("ctx")
    pencil, piece = layer_input.shape[0] // parts, layer_input.shape[1]
    length = piece * parts
    outer = length // LANES
    aligned = pencil % TILE == 0
    rows = -(-pencil // TILE) * TILE
    steps = rows // TILE
    ahead, back, back_scaled, twiddle = dft_tables(length)
    def exchange(what, blocks):
        pairs = [[(i, i ^ k) for i in range(parts)] for k in order_of(what, parts)]
        return [lax.ppermute(block, "ctx", pair) for block, pair in zip(blocks, pairs)]

    def pick(array, place):
        blocks = array.reshape(parts, pencil, piece)
        return lax.dynamic_index_in_dim(blocks, place, 0, keepdims=False)

    def pad(block):
        return block if aligned else jnp.pad(block, ((0, rows - pencil), (0, 0)))

    here = pl.BlockSpec(memory_space=pltpu.VMEM)
    there = pl.BlockSpec(memory_space=pl.ANY)
    spec_shape = jax.ShapeDtypeStruct((steps, outer * TILE, 2 * LANES), jnp.float32)
    slice_shape = jax.ShapeDtypeStruct((rows, piece), jnp.bfloat16)
    work = pltpu.VMEM((outer * TILE, 2 * LANES), jnp.float32)
    lane_tiles = pltpu.VMEM((outer, TILE, LANES), jnp.float32)
    params = pltpu.CompilerParams(vmem_limit_bytes=16 * 1024 * 1024)
    stage_flops = 2 * 3 * rows * outer * (2 * LANES) ** 2
    spec_bytes = 4 * rows * length * 2

    def cost(stages, moved):
        return pl.CostEstimate(flops=stages * stage_flops, bytes_accessed=moved, transcendentals=0)

    def in_hbm(array):
        return pltpu.with_memory_space_constraint(array, pltpu.HBM)

    own, *others = places_of("grad", parts)
    if aligned:
        count = 2 * parts - 1
        blocks = pl.pallas_call(
            functools.partial(slice_kernel, parts=parts, pencil=pencil),
            in_specs=[there] * 2,
            out_specs=[here] * count,
            out_shape=[slice_shape] * count,
            scratch_shapes=[pltpu.SemaphoreType.DMA((count,))],
            cost_estimate=cost(0, 2 * count * pencil * piece * 2),
            name="slice_blocks",
        )(in_hbm(grad_output), in_hbm(layer_input))
    else:
        blocks = [pick(grad_output, place) for place in [*others[1:], own]]
        blocks += [pick(layer_input, place) for place in places_of("input", parts)]
    grad_blocks, input_blocks = blocks[: parts - 1], blocks[parts - 1 :]
    grad_pieces = [grad_blocks[-1], *exchange("grad", [pick(grad_output, others[0]), *grad_blocks[:-1]])]
    input_pieces = [input_blocks[0], *exchange("input", input_blocks[1:])]

    taps = filter_taps.reshape(pencil, length)
    tables = [*ahead, twiddle, *back, *back_scaled]
    results = pl.pallas_call(
        functools.partial(spectrum_kernel, outer=outer, tables=len(tables)),
        in_specs=[there] * (1 + len(tables)),
        out_specs=[here] * (1 + len(tables)),
        out_shape=[spec_shape] + [jax.ShapeDtypeStruct(table.shape, table.dtype) for table in tables],
        scratch_shapes=[
            pltpu.VMEM((rows, length), jnp.float32),
            work,
            pltpu.SemaphoreType.DMA((steps + len(tables),)),
        ],
        compiler_params=params,
        cost_estimate=cost(1, 2 * spec_bytes),
        name="taps_spectrum",
    )(*map(in_hbm, [pad(taps), *map(jnp.asarray, tables)]))
    taps_spectrum, *tables = results
    ahead, twiddle, back, back_scaled = tables[:2], tables[2], tables[3:5], tables[5:]
    tables = [*ahead, *back, twiddle]
    grad_spectrum, *outgoing = pl.pallas_call(
        functools.partial(input_kernel, outer=outer, parts=parts),
        in_specs=[here] * (parts + 1 + len(tables)),
        out_specs=[here] * (parts + 1),
        out_shape=[spec_shape, *[slice_shape] * parts],
        scratch_shapes=[lane_tiles, work, lane_tiles],
        compiler_params=params,
        cost_estimate=cost(2, 2 * spec_bytes),
        name="grad_input",
    )(*map(pad, grad_pieces), taps_spectrum, *tables)

    outgoing = [block[:pencil] for block in outgoing]
    incoming = [outgoing[0], *exchange("back", outgoing[1:])]

    tables = [*ahead, *back_scaled, twiddle]
    filter_shape = jax.ShapeDtypeStruct((rows, length), jnp.float32)
    whole_shape = jax.ShapeDtypeStruct((parts * pencil, piece), jnp.bfloat16)
    grad_filter, *whole = pl.pallas_call(
        functools.partial(filter_kernel, outer=outer, parts=parts),
        in_specs=[here] * (parts + 1 + len(tables) + aligned),
        out_specs=[there] * (1 + aligned),
        out_shape=[filter_shape, whole_shape][: 1 + aligned],
        scratch_shapes=[
            lane_tiles,
            work,
            lane_tiles,
            pltpu.VMEM((rows, length), jnp.float32),
            pltpu.SemaphoreType.DMA((steps + aligned,)),
        ],
        compiler_params=params,
        cost_estimate=cost(2, 2 * spec_bytes),
        name="grad_filter",
    )(*map(pad, input_pieces), grad_spectrum, *tables, *incoming[:aligned])

    if aligned:
        (grad_input,) = whole
        for first, last in ((1, 2), (2, parts)):
            blocks = [pltpu.with_memory_space_constraint(block, pltpu.VMEM) for block in incoming[first:last]]
            grad_input = pl.pallas_call(
                functools.partial(gather_kernel, first=first, parts=parts, pencil=pencil),
                in_specs=[there] * (1 + len(blocks)),
                out_specs=there,
                out_shape=whole_shape,
                input_output_aliases={0: 0},
                scratch_shapes=[pltpu.SemaphoreType.DMA((len(blocks),))],
                name="gather_pieces",
            )(grad_input, *blocks)
    else:
        grad_input = jnp.zeros((parts, pencil, piece), jnp.bfloat16)
        for place, block in zip(places_of("back", parts), incoming):
            grad_input = lax.dynamic_update_index_in_dim(grad_input, block, place, 0)
        grad_input = grad_input.reshape(parts * pencil, piece)
    return (grad_input, grad_filter[:pencil].reshape(1, pencil, length))


def solution(mesh):
    in_specs = (P(("dp", "chan"), "ctx"), P(("dp", "chan"), "ctx"), P(("dp", "chan"), "ctx", None))
    out_specs = (P(("dp", "chan"), "ctx"), P(("dp", "chan"), "ctx", None))
    return jax.shard_map(shards, mesh=mesh, in_specs=in_specs, out_specs=out_specs, check_vma=False)
```

```python
import functools
import math

import jax
import jax.numpy as jnp
import ml_dtypes
import numpy as np
from jax import lax
from jax.experimental import pallas as pl
from jax.experimental.pallas import tpu as pltpu
from jax.sharding import PartitionSpec as P

LANES = 128
TILE = 16
HALF_TILE = 8


def split_table(table):
    high = table.astype(ml_dtypes.bfloat16)
    low = (table - high.astype(np.float64)).astype(ml_dtypes.bfloat16)
    return high, low


def dft_tables(length):
    index = np.arange(LANES)
    angle = 2.0 * np.pi * (np.outer(index, index) % LANES) / LANES
    cos, sin = np.cos(angle), np.sin(angle)
    ahead = np.block([[cos, -sin], [sin, cos]])
    back = np.block([[cos, sin], [-sin, cos]]) / length
    outer = length // LANES
    order = np.concatenate([np.arange(0, outer, 2), np.arange(1, outer, 2)])
    turn = 2.0 * np.pi * np.outer(order + 0.25, index) / length
    twiddle = np.stack([np.cos(turn), np.sin(turn)], axis=1).astype(np.float32)
    return split_table(ahead), split_table(back), split_table(back / math.sqrt(length)), twiddle


def add(a, b):
    return (a[0] + b[0], a[1] + b[1])


def sub(a, b):
    return (a[0] - b[0], a[1] - b[1])


def turn_quarter(a, sign):
    return (-a[1], a[0]) if sign > 0 else (a[1], -a[0])


def turn_by(a, numerator, denominator, sign):
    numerator = numerator % denominator
    if numerator == 0:
        return a
    if 4 * numerator == denominator:
        return turn_quarter(a, sign)
    if 2 * numerator == denominator:
        return (-a[0], -a[1])
    if 4 * numerator == 3 * denominator:
        return turn_quarter(a, -sign)
    angle = sign * 2.0 * math.pi * numerator / denominator
    cos, sin = math.cos(angle), math.sin(angle)
    if 8 * numerator % denominator == 0:
        root = math.sqrt(0.5)
        re, im = a
        if cos * sin > 0:
            re, im = re - im, re + im
        else:
            re, im = re + im, im - re
        return (re * (root if cos > 0 else -root), im * (root if cos > 0 else -root))
    return (a[0] * cos - a[1] * sin, a[0] * sin + a[1] * cos)


def fft(points, sign):
    count = len(points)
    if count == 1:
        return points
    if count == 2:
        return [add(points[0], points[1]), sub(points[0], points[1])]
    if count % 4:
        evens, odds = fft(points[0::2], sign), fft(points[1::2], sign)
        turned = [turn_by(odds[k], k, count, sign) for k in range(count // 2)]
        return [add(a, b) for a, b in zip(evens, turned)] + [sub(a, b) for a, b in zip(evens, turned)]
    quarter = count // 4
    parts = [fft(points[r::4], sign) for r in range(4)]
    out = [None] * count
    for k in range(quarter):
        p0, p1, p2, p3 = (turn_by(parts[r][k], r * k, count, sign) for r in range(4))
        s02, d02, s13, d13 = add(p0, p2), sub(p0, p2), add(p1, p3), sub(p1, p3)
        out[k] = add(s02, s13)
        out[k + 2 * quarter] = sub(s02, s13)
        if sign > 0:
            out[k + quarter] = (d02[0] - d13[1], d02[1] + d13[0])
            out[k + 3 * quarter] = (d02[0] + d13[1], d02[1] - d13[0])
        else:
            out[k + quarter] = (d02[0] + d13[1], d02[1] - d13[0])
            out[k + 3 * quarter] = (d02[0] - d13[1], d02[1] + d13[0])
    return out


def outer_forward(load, store, twiddle_ref, outer, half):
    count = outer // 2
    for row in range(0, TILE, HALF_TILE):
        points = []
        for n in range(count):
            near = -2.0 * math.pi * n * (half + 0.25) / outer
            far = -2.0 * math.pi * (n + count) * (half + 0.25) / outer
            a, b = load(n, row), load(n + count, row)
            if n == 0:
                points.append((a + b * math.cos(far), b * math.sin(far)))
            else:
                points.append((a * math.cos(near) + b * math.cos(far), a * math.sin(near) + b * math.sin(far)))
        for k, (re, im) in enumerate(fft(points, -1)):
            at = half * count + k
            cos, sin = twiddle_ref[at, 0:1, :], twiddle_ref[at, 1:2, :]
            store(at, row, re * cos + im * sin, im * cos - re * sin)


def outer_inverse(spec_ref, twiddle_ref, out_ref, outer, half):
    count = outer // 2
    for row in range(0, TILE, HALF_TILE):
        points = []
        for k in range(count):
            at = half * count + k
            rows = pl.ds(at * TILE + row, HALF_TILE)
            re, im = spec_ref[rows, 0:LANES], spec_ref[rows, LANES : 2 * LANES]
            cos, sin = twiddle_ref[at, 0:1, :], twiddle_ref[at, 1:2, :]
            points.append((re * cos - im * sin, re * sin + im * cos))
        for n, (re, im) in enumerate(fft(points, 1)):
            for place in (n, n + count):
                angle = 2.0 * math.pi * place * (half + 0.25) / outer
                value = re if place == 0 else re * math.cos(angle) - im * math.sin(angle)
                if half == 0:
                    out_ref[place, row : row + HALF_TILE, :] = value
                else:
                    out_ref[place, row : row + HALF_TILE, :] += value


def matmul(values, high_ref, low_ref):
    high = values.astype(jnp.bfloat16)
    low = (values - high.astype(jnp.float32)).astype(jnp.bfloat16)
    dot = functools.partial(jnp.dot, preferred_element_type=jnp.float32)
    both = dot(jnp.concatenate([high, low], axis=0), high_ref[...])
    count = high.shape[0]
    return both[:count] + both[count:] + dot(high, low_ref[...])


def order_of(what, parts):
    near = list(range(1, parts))
    return {"grad": near[-1:] + near[:-1], "input": near, "back": near[-1:] + near[:-1]}[what]


def places_of(what, parts):
    me = lax.axis_index("ctx")
    return [me ^ k for k in [0, *order_of(what, parts)]]


def put(work_ref, at, row, re, im):
    rows = pl.ds(at * TILE + row, HALF_TILE)
    work_ref[rows, 0:LANES] = re
    work_ref[rows, LANES : 2 * LANES] = im


def spectrum_kernel(taps_ref, *refs, outer, tables):
    table_refs, spec_ref, tables_here = refs[:tables], refs[tables], refs[tables + 1 : -3]
    taps_here, work_ref, sems = refs[-3:]
    high_here, low_here, twiddle_here = tables_here[:3]
    count = outer // 2
    steps = taps_ref.shape[0] // TILE

    def fetch(step):
        rows = pl.ds(step * TILE, TILE)
        return pltpu.make_async_copy(taps_ref.at[rows, :], taps_here.at[rows, :], sems.at[step])

    copies = [
        pltpu.make_async_copy(table_ref, here, sems.at[steps + at])
        for at, (table_ref, here) in enumerate(zip(table_refs, tables_here))
    ]
    copies, later = copies[:3], copies[3:]
    fetch(0).start()
    for copy in reversed(copies):
        copy.start()
    for step in range(1, steps):
        fetch(step).start()
    for copy in later:
        copy.start()
    for copy in copies:
        copy.wait()

    @pl.loop(0, steps)
    def _(step):
        fetch(step).wait()

        def load(n, row):
            return taps_here[pl.ds(pl.multiple_of(step * TILE + row, HALF_TILE), HALF_TILE), n * LANES : (n + 1) * LANES]

        for half in range(2):
            outer_forward(load, functools.partial(put, work_ref), twiddle_here, outer, half)
        for half in range(2):
            rows = pl.ds(half * count * TILE, count * TILE)
            spec_ref[step, rows, :] = matmul(work_ref[rows, :], high_here, low_here)

    for copy in later:
        copy.wait()


def correlate(step, piece_refs, places, mate_ref, keep_ref, signal_is_grad, tables, fill_ref, work_ref, out_ref, outer):
    ahead_high, ahead_low, back_high, back_low, twiddle_ref = tables
    count = outer // 2
    per_piece = outer // len(piece_refs)
    rows = pl.ds(pl.multiple_of(step * TILE, TILE), TILE)
    for place, ref in zip(places, piece_refs):
        first = place * per_piece
        for i in range(per_piece):
            fill_ref[first + i] = ref[rows, i * LANES : (i + 1) * LANES].astype(jnp.float32)

    def load(n, row):
        return fill_ref[n, row : row + HALF_TILE, :]

    for half in range(2):
        outer_forward(load, functools.partial(put, work_ref), twiddle_ref, outer, half)
    for half in range(2):
        rows = pl.ds(half * count * TILE, count * TILE)
        own = matmul(work_ref[rows, :], ahead_high, ahead_low)
        if keep_ref is not None:
            keep_ref[step, rows, :] = own
        mate = mate_ref[step, rows, :]
        grad, other = (own, mate) if signal_is_grad else (mate, own)
        grad_re, grad_im = grad[:, :LANES], grad[:, LANES:]
        other_re, other_im = other[:, :LANES], other[:, LANES:]
        both = jnp.concatenate(
            [other_re * grad_re + other_im * grad_im, other_re * grad_im - other_im * grad_re], axis=1
        )
        work_ref[rows, :] = matmul(both, back_high, back_low)
    for half in range(2):
        outer_inverse(work_ref, twiddle_ref, out_ref, outer, half)


def input_kernel(*refs, outer, parts):
    pieces, (mate_ref, *tables) = refs[:parts], refs[parts : parts + 6]
    keep_ref, *sends = refs[parts + 6 : 2 * parts + 7]
    fill_ref, work_ref, out_ref = refs[2 * parts + 7 :]
    places, send_places = places_of("grad", parts), places_of("back", parts)
    per_piece = outer // parts

    @pl.loop(0, pieces[0].shape[0] // TILE)
    def _(step):
        correlate(step, pieces, places, mate_ref, keep_ref, True, tables, fill_ref, work_ref, out_ref, outer)
        rows = pl.ds(pl.multiple_of(step * TILE, TILE), TILE)
        for place, ref in zip(send_places, sends):
            first = place * per_piece
            for i in range(per_piece):
                ref[rows, i * LANES : (i + 1) * LANES] = out_ref[first + i].astype(jnp.bfloat16)


def filter_kernel(*refs, outer, parts):
    pieces, (mate_ref, *tables) = refs[:parts], refs[parts : parts + 6]
    *moved, fill_ref, work_ref, out_ref, result_here, sems = refs[parts + 6 :]
    own_ref, result_ref, whole_ref = moved if len(moved) == 3 else (None, *moved, None)
    places = places_of("input", parts)
    steps = pieces[0].shape[0] // TILE
    if own_ref is not None:
        rows = pl.ds(places[0] * own_ref.shape[0], own_ref.shape[0])
        own_copy = pltpu.make_async_copy(own_ref, whole_ref.at[rows, :], sems.at[steps])
        own_copy.start()

    def flush(step):
        rows = pl.ds(pl.multiple_of(step * TILE, TILE), TILE)
        return pltpu.make_async_copy(result_here.at[rows, :], result_ref.at[rows, :], sems.at[step])

    @pl.loop(0, steps)
    def _(step):
        correlate(step, pieces, places, mate_ref, None, False, tables, fill_ref, work_ref, out_ref, outer)
        rows = pl.ds(pl.multiple_of(step * TILE, TILE), TILE)
        for n in range(outer):
            result_here[rows, n * LANES : (n + 1) * LANES] = out_ref[n]
        flush(step).start()

    @pl.loop(0, steps)
    def _(step):
        flush(step).wait()

    if own_ref is not None:
        own_copy.wait()


def slice_kernel(grad_ref, input_ref, *refs, parts, pencil):
    *blocks, sems = refs
    grad_places, input_places = places_of("grad", parts), places_of("input", parts)
    moves = [(grad_ref, place) for place in grad_places[2:] + grad_places[:1]]
    moves += [(input_ref, place) for place in input_places]
    copies = []
    for (source_ref, place), ref in zip(moves, blocks):
        rows = pl.ds(place * pencil, pencil)
        copies.append(pltpu.make_async_copy(source_ref.at[rows, :], ref, sems.at[len(copies)]))
    for copy in copies:
        copy.start()
    for copy in copies:
        copy.wait()


def gather_kernel(held_ref, *refs, first, parts, pencil):
    *pieces, out_ref, sems = refs
    copies = []
    for place, ref in zip(places_of("back", parts)[first:], pieces):
        rows = pl.ds(place * pencil, pencil)
        copies.append(pltpu.make_async_copy(ref, out_ref.at[rows, :], sems.at[len(copies)]))
    for copy in copies:
        copy.start()
    for copy in copies:
        copy.wait()


def shards(layer_input, grad_output, filter_taps):
    parts = lax.axis_size("ctx")
    pencil, piece = layer_input.shape[0] // parts, layer_input.shape[1]
    length = piece * parts
    outer = length // LANES
    aligned = pencil % TILE == 0
    rows = -(-pencil // TILE) * TILE
    steps = rows // TILE
    ahead, back, back_scaled, twiddle = dft_tables(length)
    def exchange(what, blocks):
        pairs = [[(i, i ^ k) for i in range(parts)] for k in order_of(what, parts)]
        return [lax.ppermute(block, "ctx", pair) for block, pair in zip(blocks, pairs)]

    def pick(array, place):
        blocks = array.reshape(parts, pencil, piece)
        return lax.dynamic_index_in_dim(blocks, place, 0, keepdims=False)

    def pad(block):
        return block if aligned else jnp.pad(block, ((0, rows - pencil), (0, 0)))

    here = pl.BlockSpec(memory_space=pltpu.VMEM)
    there = pl.BlockSpec(memory_space=pl.ANY)
    spec_shape = jax.ShapeDtypeStruct((steps, outer * TILE, 2 * LANES), jnp.float32)
    slice_shape = jax.ShapeDtypeStruct((rows, piece), jnp.bfloat16)
    work = pltpu.VMEM((outer * TILE, 2 * LANES), jnp.float32)
    lane_tiles = pltpu.VMEM((outer, TILE, LANES), jnp.float32)
    params = pltpu.CompilerParams(vmem_limit_bytes=16 * 1024 * 1024)
    stage_flops = 2 * 3 * rows * outer * (2 * LANES) ** 2
    spec_bytes = 4 * rows * length * 2

    def cost(stages, moved):
        return pl.CostEstimate(flops=stages * stage_flops, bytes_accessed=moved, transcendentals=0)

    def in_hbm(array):
        return pltpu.with_memory_space_constraint(array, pltpu.HBM)

    own, *others = places_of("grad", parts)
    if aligned:
        count = 2 * parts - 1
        blocks = pl.pallas_call(
            functools.partial(slice_kernel, parts=parts, pencil=pencil),
            in_specs=[there] * 2,
            out_specs=[here] * count,
            out_shape=[slice_shape] * count,
            scratch_shapes=[pltpu.SemaphoreType.DMA((count,))],
            cost_estimate=cost(0, 2 * count * pencil * piece * 2),
            name="slice_blocks",
        )(in_hbm(grad_output), in_hbm(layer_input))
    else:
        blocks = [pick(grad_output, place) for place in [*others[1:], own]]
        blocks += [pick(layer_input, place) for place in places_of("input", parts)]
    grad_blocks, input_blocks = blocks[: parts - 1], blocks[parts - 1 :]
    grad_pieces = [grad_blocks[-1], *exchange("grad", [pick(grad_output, others[0]), *grad_blocks[:-1]])]
    input_pieces = [input_blocks[0], *exchange("input", input_blocks[1:])]

    taps = filter_taps.reshape(pencil, length)
    tables = [*ahead, twiddle, *back, *back_scaled]
    results = pl.pallas_call(
        functools.partial(spectrum_kernel, outer=outer, tables=len(tables)),
        in_specs=[there] * (1 + len(tables)),
        out_specs=[here] * (1 + len(tables)),
        out_shape=[spec_shape] + [jax.ShapeDtypeStruct(table.shape, table.dtype) for table in tables],
        scratch_shapes=[
            pltpu.VMEM((rows, length), jnp.float32),
            work,
            pltpu.SemaphoreType.DMA((steps + len(tables),)),
        ],
        compiler_params=params,
        cost_estimate=cost(1, 2 * spec_bytes),
        name="taps_spectrum",
    )(*map(in_hbm, [pad(taps), *map(jnp.asarray, tables)]))
    taps_spectrum, *tables = results
    ahead, twiddle, back, back_scaled = tables[:2], tables[2], tables[3:5], tables[5:]
    tables = [*ahead, *back, twiddle]
    grad_spectrum, *outgoing = pl.pallas_call(
        functools.partial(input_kernel, outer=outer, parts=parts),
        in_specs=[here] * (parts + 1 + len(tables)),
        out_specs=[here] * (parts + 1),
        out_shape=[spec_shape, *[slice_shape] * parts],
        scratch_shapes=[lane_tiles, work, lane_tiles],
        compiler_params=params,
        cost_estimate=cost(2, 2 * spec_bytes),
        name="grad_input",
    )(*map(pad, grad_pieces), taps_spectrum, *tables)

    outgoing = [block[:pencil] for block in outgoing]
    incoming = [outgoing[0], *exchange("back", outgoing[1:])]

    tables = [*ahead, *back_scaled, twiddle]
    filter_shape = jax.ShapeDtypeStruct((rows, length), jnp.float32)
    whole_shape = jax.ShapeDtypeStruct((parts * pencil, piece), jnp.bfloat16)
    grad_filter, *whole = pl.pallas_call(
        functools.partial(filter_kernel, outer=outer, parts=parts),
        in_specs=[here] * (parts + 1 + len(tables) + aligned),
        out_specs=[there] * (1 + aligned),
        out_shape=[filter_shape, whole_shape][: 1 + aligned],
        scratch_shapes=[
            lane_tiles,
            work,
            lane_tiles,
            pltpu.VMEM((rows, length), jnp.float32),
            pltpu.SemaphoreType.DMA((steps + aligned,)),
        ],
        compiler_params=params,
        cost_estimate=cost(2, 2 * spec_bytes),
        name="grad_filter",
    )(*map(pad, input_pieces), grad_spectrum, *tables, *incoming[:aligned])

    if aligned:
        (grad_input,) = whole
        for first, last in ((1, 2), (2, parts)):
            blocks = [pltpu.with_memory_space_constraint(block, pltpu.VMEM) for block in incoming[first:last]]
            grad_input = pl.pallas_call(
                functools.partial(gather_kernel, first=first, parts=parts, pencil=pencil),
                in_specs=[there] * (1 + len(blocks)),
                out_specs=there,
                out_shape=whole_shape,
                input_output_aliases={0: 0},
                scratch_shapes=[pltpu.SemaphoreType.DMA((len(blocks),))],
                name="gather_pieces",
            )(grad_input, *blocks)
    else:
        grad_input = jnp.zeros((parts, pencil, piece), jnp.bfloat16)
        for place, block in zip(places_of("back", parts), incoming):
            grad_input = lax.dynamic_update_index_in_dim(grad_input, block, place, 0)
        grad_input = grad_input.reshape(parts * pencil, piece)
    return (grad_input, grad_filter[:pencil].reshape(1, pencil, length))


def solution(mesh):
    in_specs = (P(("dp", "chan"), "ctx"), P(("dp", "chan"), "ctx"), P(("dp", "chan"), "ctx", None))
    out_specs = (P(("dp", "chan"), "ctx"), P(("dp", "chan"), "ctx", None))
    return jax.shard_map(shards, mesh=mesh, in_specs=in_specs, out_specs=out_specs, check_vma=False)
```
